32 devices in a mesh: seq: 8 (over z, y), tp: 4 (over x, core).
Axes of the slice: x: 2, y: 2, z: 4, core: 2. Of those that a mesh axis runs over, the one named last changes fastest.
Arguments:
- probe_vectors: bfloat16 [4096, 8192], P('seq', 'tp'), may hold values from -6 to 6
- lookup_vectors: bfloat16 [4096, 8192], P('seq', 'tp'), may hold values from -0.5 to 0.5
- payload_vectors: bfloat16 [4096, 8192], P('seq', 'tp'), may hold values from -400 to 400
- attender_fading_pace: float32 [64], P('tp'), may hold values from 0 to 0.034, as said below
- surplus_fading: float32 [4096, 64], P('seq', 'tp'), may hold values from -0.7 to 0, as said below
- normalizer_scaling: float32 [8192], P('tp'), may hold values from 0.25 to 1.75
Outputs:
- attended: bfloat16 [4096, 8192], P('seq', 'tp')
- final_state: float32 [64, 16384], P('tp', 'seq')
The draws below stay inside these ranges and needn't reach their ends.
Inputs may be any that keep to these rules, and one draw needn't show every extreme that they name: `attender_fading_pace`: positive per-token decay rates; some heads forget within some tens of tokens. `surplus_fading`: zero at most tokens.
All inputs are finite; a program needn't handle non-finite values.
Results may differ from the reference program's by a relative error of at most 0.0031.
Values sent between devices are 32-bit elements; how exact they have to be, the bound alone decides.
A program may use at most 192 MiB of HBM per device.

```python
import math
import jax
import jax.numpy as jnp
from jax import lax

HEADS = 64
HEAD_DIM = 128
BLOCK = 256
D = 8192
TOKENS = 4096


def draw_payload_vectors(key, part):
    first, second_operand = jax.random.split(key, 2)
    base = jnp.clip(jax.random.normal(first, (TOKENS, D), jnp.float32), -4.0, 4.0)
    column = jnp.exp(jax.random.uniform(second_operand, (1, D), jnp.float32, 0.0, math.log(10.0)))
    return (base * column).astype(jnp.bfloat16)


def draw_attender_fading_pace(key, part):
    key_choice, key_slow, key_medium, key_fast, key_quick = jax.random.split(key, 5)
    slow_share = 0.5
    medium_share = 0.65
    fast_share = 0.88
    picker = jax.random.uniform(key_choice, (HEADS,), jnp.float32)
    slow_rates = jnp.exp(jax.random.uniform(key_slow, (HEADS,), jnp.float32, math.log(0.05), math.log(0.8))) / TOKENS
    medium_rates = jnp.exp(jax.random.uniform(key_medium, (HEADS,), jnp.float32, math.log(0.0002), math.log(0.00039)))
    fast_rates = jax.random.uniform(key_fast, (HEADS,), jnp.float32, 0.0098, 0.0125)
    quick_rates = jnp.exp(jax.random.uniform(key_quick, (HEADS,), jnp.float32, math.log(1.0 / 50.0), math.log(1.0 / 30.0)))
    rates = jnp.where(picker < slow_share, slow_rates, jnp.where(picker < medium_share, medium_rates, jnp.where(picker < fast_share, fast_rates, quick_rates)))
    return rates.astype(jnp.float32)


def draw_surplus_fading(key, part):
    first, second_operand = jax.random.split(key, 2)
    hits = jax.random.uniform(first, (TOKENS, HEADS), jnp.float32) < 2.0 / TOKENS
    depth = jnp.log(jax.random.uniform(second_operand, (TOKENS, HEADS), jnp.float32, 0.5, 0.8))
    return jnp.where(hits, depth, 0.0).astype(jnp.float32)


def block_levels(stream_key, dims, shards, low, top_value):
    factor_of = 1.0
    for axis_at, parts in shards:
        draws = jax.random.uniform(jax.random.fold_in(jax.random.fold_in(stream_key, 6), axis_at), (parts,), jnp.float32, low / len(shards), top_value / len(shards))
        factor_of = factor_of * jnp.repeat(jnp.exp(draws), dims[axis_at] // parts).reshape((-1,) + (1,) * (len(dims) - 1 - axis_at))
    return factor_of


def normal_values(own_key, extent, width, limit, pieces=(), held_as=jnp.bfloat16):
    result = width * jax.random.normal(own_key, extent, jnp.float32)
    if pieces:
        result = result * block_levels(own_key, extent, pieces, -0.22, 0.18)
    return jnp.clip(result, -limit, limit).astype(held_as)


def setup_inputs(seed: int = 0) -> dict:
    seeds = jax.random.split(jax.random.key(seed), 7)
    probe_vectors = normal_values(seeds[0], (TOKENS, D), 1.0, 6.0, ((0, 8), (1, 4)))
    lookup_vectors = normal_values(seeds[1], (TOKENS, D), HEAD_DIM ** -0.5, 0.5, ((0, 8), (1, 4)))
    payload_vectors = draw_payload_vectors(jax.random.fold_in(seeds[6], 71), 0)
    attender_fading_pace = draw_attender_fading_pace(jax.random.fold_in(seeds[6], 71), 0)
    surplus_fading = draw_surplus_fading(jax.random.fold_in(seeds[6], 71), 0)
    normalizer_scaling = jnp.clip(1.0 + 0.15 * jax.random.normal(seeds[5], (D,), jnp.float32), 0.25, 1.75)
    return {"probe_vectors": probe_vectors, "lookup_vectors": lookup_vectors, "payload_vectors": payload_vectors, "attender_fading_pace": attender_fading_pace, "surplus_fading": surplus_fading, "normalizer_scaling": normalizer_scaling}


def block_update(qb, kb, vb, gb, state):
    c = jnp.cumsum(gb, axis=0)
    qf = qb.astype(jnp.float32)
    kf = kb.astype(jnp.float32)
    vf = vb.astype(jnp.float32)
    scores = jnp.einsum('thd,shd->hts', qf, kf, precision=lax.Precision.HIGHEST)
    trans = c.T
    diff = trans[:, :, None] - trans[:, None, :]
    size = c.shape[0]
    lower = jnp.arange(size)[:, None] >= jnp.arange(size)[None, :]
    factor = jnp.where(lower[None, :, :], jnp.exp(jnp.minimum(diff, 0.0)), 0.0)
    rounded = lax.optimization_barrier((scores * factor).astype(jnp.bfloat16)).astype(jnp.float32)
    intra = jnp.einsum('hts,shd->thd', rounded, vf, precision=lax.Precision.HIGHEST)
    inter = jnp.exp(c)[:, :, None] * jnp.einsum('thd,hde->the', qf, state, precision=lax.Precision.HIGHEST)
    last = c[-1]
    decayed = kf * jnp.exp(last[None, :] - c)[:, :, None]
    fresh = jnp.exp(last)[:, None, None] * state + jnp.einsum('thd,the->hde', decayed, vf, precision=lax.Precision.HIGHEST)
    return (intra + inter, fresh)

def reference(probe_vectors, lookup_vectors, payload_vectors, attender_fading_pace, surplus_fading, normalizer_scaling):
    block_list = TOKENS // BLOCK
    exponent_of_fading = surplus_fading - attender_fading_pace[None, :]
    shaped = lambda arr: arr.reshape(block_list, BLOCK, HEADS, HEAD_DIM)

    def step(state, input_arrays):
        qb, kb, vb, gb = input_arrays
        out, fresh = block_update(qb, kb, vb, gb, state)
        return (fresh, out)
    start = jnp.zeros((HEADS, HEAD_DIM, HEAD_DIM), jnp.float32)
    final, outs = lax.scan(step, start, (shaped(probe_vectors), shaped(lookup_vectors), shaped(payload_vectors), exponent_of_fading.reshape(block_list, BLOCK, HEADS)))
    merged = outs.reshape(TOKENS, D)
    meansq = lax.optimization_barrier(jnp.sum(merged * merged, axis=1, keepdims=True)) / D
    attended = (merged * lax.rsqrt(meansq + 1e-06) * normalizer_scaling[None, :]).astype(jnp.bfloat16)
    return (attended, final.reshape(HEADS, HEAD_DIM * HEAD_DIM))
```

```python
import functools

import jax
import jax.numpy as jnp
from jax import lax
from jax.experimental import pallas as pl
from jax.experimental.pallas import tpu as pltpu
from jax.sharding import PartitionSpec as P

HEAD_DIM = 128
HALF = HEAD_DIM // 2
BLOCK = 256
D = 8192
EPS = 1e-06
F32 = jnp.float32
BF16 = jnp.bfloat16
MESH = pl.DeviceIdType.MESH


def split(x, axis):
    high = x.astype(BF16)
    low = (x - high.astype(F32)).astype(BF16)
    return jnp.concatenate([high, low], axis=axis)


def kernel(
    n, peers, heads, group,
    q_hbm, k_hbm, v_hbm, pace_ref, surplus_ref, gain_ref,
    out_hbm, final_ref,
    qs, ks, vs, outs, acc, col, crow, first, local, theirs, prior, before, after, give,
    dec, dec_theirs, fsend, frecv, squares,
    load_sem, store_sem, dec_sem, l_send, l_recv, p_send, p_recv, x_send, x_recv,
    f_send, f_recv, s_send, s_recv,
):
    tokens = q_hbm.shape[0]
    blocks = tokens // BLOCK
    chunks = heads // group
    wide = group * HEAD_DIM
    groups = n // 2
    rows = HEAD_DIM // n
    me = lax.axis_index("seq")
    place = lax.axis_index("tp")
    g, r = me // 2, me % 2
    other = 1 - r
    partner = 2 * g + other
    is_first, is_last = g == 0, g == groups - 1

    barrier = pltpu.get_barrier_semaphore()
    for step in range(1, n):
        pl.semaphore_signal(
            barrier, inc=1, device_id={"seq": lax.rem(me + step, n)}, device_id_type=MESH
        )
    for step in range(1, peers):
        pl.semaphore_signal(
            barrier, inc=1, device_id={"tp": lax.rem(place + step, peers)}, device_id_type=MESH
        )

    def lanes(i):
        return pl.ds(pl.multiple_of(i * wide, wide), wide)

    def load(which, i):
        source = (k_hbm, v_hbm, q_hbm)[which]
        target = (ks, vs, qs)[which]
        return pltpu.make_async_copy(
            source.at[:, lanes(i)], target.at[i], load_sem.at[which, i]
        )

    def store(i):
        return pltpu.make_async_copy(outs.at[i], out_hbm.at[:, lanes(i)], store_sem.at[i])

    def span(i):
        return pl.ds(i * group, group)

    def send_dec():
        return pltpu.make_async_remote_copy(
            src_ref=dec, dst_ref=dec_theirs, send_sem=dec_sem.at[0], recv_sem=dec_sem.at[1],
            device_id={"seq": partner}, device_id_type=MESH,
        )

    def send_local(i):
        return pltpu.make_async_remote_copy(
            src_ref=local.at[other, span(i)], dst_ref=theirs.at[span(i)],
            send_sem=l_send.at[i], recv_sem=l_recv.at[i],
            device_id={"seq": partner}, device_id_type=MESH,
        )

    def send_after(i):
        return pltpu.make_async_remote_copy(
            src_ref=after.at[span(i)], dst_ref=before.at[span(i)],
            send_sem=p_send.at[i], recv_sem=p_recv.at[i],
            device_id={"seq": lax.rem(me + 2, n)}, device_id_type=MESH,
        )

    def send_prior(i):
        return pltpu.make_async_remote_copy(
            src_ref=give.at[span(i)], dst_ref=prior.at[r, span(i)],
            send_sem=x_send.at[i], recv_sem=x_recv.at[i],
            device_id={"seq": partner}, device_id_type=MESH,
        )

    def send_final(i, s):
        return pltpu.make_async_remote_copy(
            src_ref=fsend.at[s, span(i)], dst_ref=frecv.at[span(i)],
            send_sem=f_send.at[i, s], recv_sem=f_recv.at[i],
            device_id={"seq": r * groups + s}, device_id_type=MESH,
        )

    def send_squares(step):
        return pltpu.make_async_remote_copy(
            src_ref=squares.at[0], dst_ref=squares.at[step],
            send_sem=s_send.at[step], recv_sem=s_recv.at[step],
            device_id={"tp": lax.rem(place + step, peers)}, device_id_type=MESH,
        )

    for i in range(chunks):
        load(0, i).start()
        load(1, i).start()
    for i in range(chunks):
        load(2, i).start()

    logdec = surplus_ref[...] - pace_ref[...]
    upper = (
        lax.broadcasted_iota(jnp.int32, (BLOCK, BLOCK), 0)
        <= lax.broadcasted_iota(jnp.int32, (BLOCK, BLOCK), 1)
    ).astype(F32)
    logrows = logdec.T
    total = jnp.zeros((heads, 1), F32)
    for b in range(blocks):
        c = lax.dot_general(
            logrows[:, b * BLOCK : (b + 1) * BLOCK], upper, (((1,), (0,)), ((), ())),
            precision=lax.Precision.HIGHEST, preferred_element_type=F32,
        )
        crow[:, b * BLOCK : (b + 1) * BLOCK] = c
        total = total + c[:, BLOCK - 1 :]
    decay = jnp.exp(jnp.broadcast_to(total, (heads, HEAD_DIM)))
    for h in range(heads):
        dec[h] = decay[h : h + 1, :]

    @pl.when(is_first)
    def _():
        before[...] = jnp.zeros_like(before)

        @pl.when(r == 0)
        def _():
            prior[1] = jnp.zeros(prior.shape[1:], F32)

    pl.semaphore_wait(barrier, n + peers - 2)
    send_dec().start()

    def make_local(i, carry):
        load(0, i).wait()
        load(1, i).wait()
        for e in range(group):
            h = i * group + e
            row = crow[pl.ds(h, 1), :]
            column = jnp.broadcast_to(row, (HEAD_DIM, tokens)).T
            col[h] = column
            state = None
            for b in range(blocks):
                at = slice(b * BLOCK, (b + 1) * BLOCK)
                c = column[at]
                last = c[BLOCK - 1 :, :]
                kb = ks[i, at, e * HEAD_DIM : (e + 1) * HEAD_DIM]
                vb = vs[i, at, e * HEAD_DIM : (e + 1) * HEAD_DIM].astype(F32)
                pair = lax.dot_general(
                    kb, split(vb * jnp.exp(last - c), 1), (((0,), (0,)), ((), ())),
                    preferred_element_type=F32,
                )
                fresh = pair[:, :HEAD_DIM] + pair[:, HEAD_DIM:]
                state = fresh if b == 0 else jnp.exp(last) * state + fresh
                if b < blocks - 1:
                    first[b, h] = state
            local[0, h] = state[:HALF]
            local[1, h] = state[HALF:]
        send_local(i).start()
        return carry

    lax.fori_loop(0, chunks, make_local, 0)
    send_dec().wait_recv()

    def chain(i):
        send_local(i).wait_recv()

        @pl.when(jnp.logical_not(is_first))
        def _():
            send_after(i).wait_recv()

        at = span(i)
        mine, their = local[r, at], theirs[at]
        d_mine, d_their = dec[at], dec_theirs[at]
        came = before[at]
        even = r == 0
        grown = d_mine * d_their * came + jnp.where(
            even, d_their * mine + their, d_mine * their + mine
        )
        after[at] = grown

        @pl.when(jnp.logical_not(is_last))
        def _():
            send_after(i).start()

        prior[r, at] = jnp.where(even, came, d_their * came + their)

        give[at] = jnp.where(even, d_mine * came + mine, came)

        @pl.when(jnp.logical_not(is_first & (r == 1)))
        def _():
            send_prior(i).start()

        @pl.when(is_last)
        def _():
            for s in range(groups):
                fsend[s, at] = grown[:, s * rows : (s + 1) * rows, :]

            def give_final(s, carry):
                @pl.when(r * groups + s != me)
                def _():
                    send_final(i, s).start()

                @pl.when(r * groups + s == me)
                def _():
                    frecv[at] = fsend[s, at]

                return carry

            lax.fori_loop(0, groups, give_final, 0)

    lower = lax.broadcasted_iota(jnp.int32, (BLOCK, BLOCK), 0) >= lax.broadcasted_iota(
        jnp.int32, (BLOCK, BLOCK), 1
    )

    def intra(i):
        load(2, i).wait()
        for e in range(group):
            h = i * group + e
            cut = slice(e * HEAD_DIM, (e + 1) * HEAD_DIM)
            row = crow[pl.ds(h, 1), :]
            for b in range(blocks):
                at = slice(b * BLOCK, (b + 1) * BLOCK)
                c = col[h, at, :]
                scores = lax.dot_general(
                    qs[i, at, cut], ks[i, at, cut], (((1,), (1,)), ((), ())),
                    preferred_element_type=F32,
                )
                diff = jnp.concatenate([c] * (BLOCK // HEAD_DIM), axis=1) - row[:, at]
                factor = jnp.where(lower, jnp.exp(jnp.minimum(diff, 0.0)), 0.0)
                acc[h, at, :] = jnp.dot(
                    (scores * factor).astype(BF16), vs[i, at, cut], preferred_element_type=F32
                )

    lag = jnp.minimum(g, chunks)

    def middle(j, carry):
        @pl.when((j >= lag) & (j - lag < chunks))
        def _():
            chain(j - lag)

        @pl.when(j < chunks)
        def _():
            intra(j)

        return carry

    lax.fori_loop(0, chunks + min(groups - 1, chunks), middle, 0)

    def carried(i, sums):
        @pl.when(jnp.logical_not(is_first & (r == 0)))
        def _():
            send_prior(i).wait_recv()

        for e in range(group):
            h = i * group + e
            cut = slice(e * HEAD_DIM, (e + 1) * HEAD_DIM)
            start = jnp.concatenate([prior[0, h], prior[1, h]], axis=0)
            decayed = None
            parts = []
            for b in range(blocks):
                at = slice(b * BLOCK, (b + 1) * BLOCK)
                if b == 0:
                    state = start
                else:
                    state = decayed * start + first[b - 1, h]
                grow = jnp.exp(col[h, at, :])
                last = grow[BLOCK - 1 :, :]
                decayed = last if b == 0 else decayed * last
                qb = qs[i, at, cut]
                inter = jnp.dot(
                    jnp.concatenate([qb, qb], axis=1), split(state, 0),
                    preferred_element_type=F32,
                )
                out = acc[h, at, :] + grow * inter
                acc[h, at, :] = out
                parts.append(out * out)
            sums = sums + jnp.concatenate(parts, axis=0)
        return sums

    sums = lax.fori_loop(0, chunks, carried, jnp.zeros((tokens, HEAD_DIM), F32))
    squares[0] = jnp.sum(sums.T, axis=0, keepdims=True)
    for step in range(1, peers):
        send_squares(step).start()
    for step in range(1, peers):
        send_squares(step).wait_recv()
    whole = squares[0]
    for step in range(1, peers):
        whole = whole + squares[step]
    scale = lax.rsqrt(whole / D + EPS)
    scale = jnp.broadcast_to(scale, (HEAD_DIM, tokens)).T

    def finish(i, carry):
        for e in range(group):
            h = i * group + e
            gain = gain_ref[:, pl.ds(pl.multiple_of(h * HEAD_DIM, HEAD_DIM), HEAD_DIM)]
            outs[i, :, e * HEAD_DIM : (e + 1) * HEAD_DIM] = (acc[h] * scale * gain).astype(BF16)
        store(i).start()
        return carry

    lax.fori_loop(0, chunks, finish, 0)

    def drain(i, carry):
        send_local(i).wait_send()

        @pl.when(jnp.logical_not(is_last))
        def _():
            send_after(i).wait_send()

        @pl.when(jnp.logical_not(is_first & (r == 1)))
        def _():
            send_prior(i).wait_send()

        @pl.when(is_last)
        def _():
            def sent(s, carry):
                @pl.when(r * groups + s != me)
                def _():
                    send_final(i, s).wait_send()

                return carry

            lax.fori_loop(0, groups, sent, 0)

        @pl.when(me != n - 1)
        def _():
            send_final(i, 0).wait_recv()

        store(i).wait()
        return carry

    lax.fori_loop(0, chunks, drain, 0)
    send_dec().wait_send()
    for step in range(1, peers):
        send_squares(step).wait_send()
    final_ref[...] = frecv[...]


def on_device(n, peers, q, k, v, pace, surplus, gain):
    tokens, width = q.shape
    heads = pace.shape[0]
    group = 2
    chunks = heads // group
    blocks = tokens // BLOCK
    groups = n // 2
    rows = HEAD_DIM // n
    vmem = pltpu.VMEM
    dma = pltpu.SemaphoreType.DMA
    half = (heads, HALF, HEAD_DIM)
    flops = 2 * heads * tokens * HEAD_DIM * (2 * BLOCK + 4 * HEAD_DIM)
    attended, final = pl.pallas_call(
        functools.partial(kernel, n, peers, heads, group),
        out_shape=(
            jax.ShapeDtypeStruct((tokens, width), BF16),
            jax.ShapeDtypeStruct((heads, rows, HEAD_DIM), F32),
        ),
        in_specs=[pl.BlockSpec(memory_space=pl.ANY)] * 3
        + [pl.BlockSpec(memory_space=pltpu.VMEM)] * 3,
        out_specs=(
            pl.BlockSpec(memory_space=pl.ANY),
            pl.BlockSpec(memory_space=pltpu.VMEM),
        ),
        scratch_shapes=[
            vmem((chunks, tokens, group * HEAD_DIM), BF16),
            vmem((chunks, tokens, group * HEAD_DIM), BF16),
            vmem((chunks, tokens, group * HEAD_DIM), BF16),
            vmem((chunks, tokens, group * HEAD_DIM), BF16),
            vmem((heads, tokens, HEAD_DIM), F32),
            vmem((heads, tokens, HEAD_DIM), F32),
            vmem((heads, tokens), F32),
            vmem((max(blocks - 1, 1), heads, HEAD_DIM, HEAD_DIM), F32),
            vmem((2,) + half, F32),
            vmem(half, F32),
            vmem((2,) + half, F32),
            vmem(half, F32),
            vmem(half, F32),
            vmem(half, F32),
            vmem((heads, 1, HEAD_DIM), F32),
            vmem((heads, 1, HEAD_DIM), F32),
            vmem((groups, heads, rows, HEAD_DIM), F32),
            vmem((heads, rows, HEAD_DIM), F32),
            vmem((peers, 1, tokens), F32),
            dma((3, chunks)),
            dma((chunks,)),
            dma((2,)),
            dma((chunks,)),
            dma((chunks,)),
            dma((chunks,)),
            dma((chunks,)),
            dma((chunks,)),
            dma((chunks,)),
            dma((chunks, groups)),
            dma((chunks,)),
            dma((peers,)),
            dma((peers,)),
        ],
        compiler_params=pltpu.CompilerParams(
            collective_id=0, has_side_effects=True, vmem_limit_bytes=56 * 1024 * 1024
        ),
        cost_estimate=pl.CostEstimate(
            flops=flops, bytes_accessed=8 * tokens * width, transcendentals=heads * tokens * BLOCK
        ),
        name="chained_attention",
    )(q, k, v, pace.reshape(1, heads), surplus, gain.reshape(1, width))
    return attended, final.reshape(heads, rows * HEAD_DIM)


def solution(mesh):
    in_specs = (P("seq", "tp"), P("seq", "tp"), P("seq", "tp"), P("tp"), P("seq", "tp"), P("tp"))
    out_specs = (P("seq", "tp"), P("tp", "seq"))
    return jax.shard_map(
        functools.partial(on_device, mesh.shape["seq"], mesh.shape["tp"]),
        mesh=mesh, in_specs=in_specs, out_specs=out_specs, check_vma=False,
    )
```

```python
import functools

import jax
import jax.numpy as jnp
from jax import lax
from jax.experimental import pallas as pl
from jax.experimental.pallas import tpu as pltpu
from jax.sharding import PartitionSpec as P

HEAD_DIM = 128
HALF = HEAD_DIM // 2
BLOCK = 256
D = 8192
EPS = 1e-06
LOG2E = 1.4426950408889634
F32 = jnp.float32
BF16 = jnp.bfloat16
MESH = pl.DeviceIdType.MESH


def split(x, axis):
    high = x.astype(BF16)
    low = (x - high.astype(F32)).astype(BF16)
    return jnp.concatenate([high, low], axis=axis)


def kernel(
    n, peers, heads, group,
    q_hbm, k_hbm, v_hbm, pace_ref, surplus_ref, gain_ref,
    out_hbm, final_ref,
    qs, ks, vs, outs, acc, crow, erow, krow, dblock, first, local, theirs, prior, before, after, give,
    dec, dec_theirs, fsend, frecv, squares,
    load_sem, store_sem, dec_sem, l_send, l_recv, p_send, p_recv, x_send, x_recv,
    f_send, f_recv, s_send, s_recv,
):
    tokens = q_hbm.shape[0]
    blocks = tokens // BLOCK
    chunks = heads // group
    wide = group * HEAD_DIM
    groups = n // 2
    rows = HEAD_DIM // n
    piece = max(rows, 8)
    me = lax.axis_index("seq")
    place = lax.axis_index("tp")
    g, r = me // 2, me % 2
    other = 1 - r
    partner = 2 * g + other

    def owner(s):
        top = s * rows
        return ((top // piece) * 2 * piece + r * piece + top % piece) // rows

    def halves(x):
        return [
            jnp.concatenate(
                [x[at : at + piece] for at in range(p * piece, HEAD_DIM, 2 * piece)], axis=0
            )
            for p in range(2)
        ]

    def joined(a, b):
        return jnp.concatenate(
            [x[at : at + piece] for at in range(0, HALF, piece) for x in (a, b)], axis=0
        )

    is_first, is_last = g == 0, g == groups - 1

    barrier = pltpu.get_barrier_semaphore()
    for step in range(1, n):
        pl.semaphore_signal(
            barrier, inc=1, device_id={"seq": lax.rem(me + step, n)}, device_id_type=MESH
        )
    for step in range(1, peers):
        pl.semaphore_signal(
            barrier, inc=1, device_id={"tp": lax.rem(place + step, peers)}, device_id_type=MESH
        )

    def lanes(i):
        return pl.ds(pl.multiple_of(i * wide, wide), wide)

    def load(which, i):
        source = (k_hbm, v_hbm, q_hbm)[which]
        target = (ks, vs, qs)[which]
        return pltpu.make_async_copy(
            source.at[:, lanes(i)], target.at[i], load_sem.at[which, i]
        )

    def store(i):
        return pltpu.make_async_copy(outs.at[i], out_hbm.at[:, lanes(i)], store_sem.at[i])

    def span(i):
        return pl.ds(i * group, group)

    def send_dec():
        return pltpu.make_async_remote_copy(
            src_ref=dec, dst_ref=dec_theirs, send_sem=dec_sem.at[0], recv_sem=dec_sem.at[1],
            device_id={"seq": partner}, device_id_type=MESH,
        )

    def send_local(i):
        return pltpu.make_async_remote_copy(
            src_ref=local.at[other, span(i)], dst_ref=theirs.at[span(i)],
            send_sem=l_send.at[i], recv_sem=l_recv.at[i],
            device_id={"seq": partner}, device_id_type=MESH,
        )

    def send_after(i):
        return pltpu.make_async_remote_copy(
            src_ref=after.at[span(i)], dst_ref=before.at[span(i)],
            send_sem=p_send.at[i], recv_sem=p_recv.at[i],
            device_id={"seq": lax.rem(me + 2, n)}, device_id_type=MESH,
        )

    def send_prior(i):
        return pltpu.make_async_remote_copy(
            src_ref=give.at[span(i)], dst_ref=prior.at[r, span(i)],
            send_sem=x_send.at[i], recv_sem=x_recv.at[i],
            device_id={"seq": partner}, device_id_type=MESH,
        )

    def send_final(i, s):
        return pltpu.make_async_remote_copy(
            src_ref=fsend.at[s, span(i)], dst_ref=frecv.at[span(i)],
            send_sem=f_send.at[i, s], recv_sem=f_recv.at[i],
            device_id={"seq": owner(s)}, device_id_type=MESH,
        )

    def send_squares(step):
        return pltpu.make_async_remote_copy(
            src_ref=squares.at[0], dst_ref=squares.at[step],
            send_sem=s_send.at[step], recv_sem=s_recv.at[step],
            device_id={"tp": lax.rem(place + step, peers)}, device_id_type=MESH,
        )

    for i in range(chunks):
        load(0, i).start()
        load(1, i).start()
    for i in range(chunks):
        load(2, i).start()

    square = (heads, heads)
    diagonal = lax.broadcasted_iota(jnp.int32, square, 0) == lax.broadcasted_iota(
        jnp.int32, square, 1
    )
    pace = jnp.sum(
        jnp.where(diagonal, jnp.broadcast_to(pace_ref[...], square), 0.0), axis=1, keepdims=True
    )
    logrows = surplus_ref[...] - pace
    upper = (
        lax.broadcasted_iota(jnp.int32, (BLOCK, BLOCK), 0)
        <= lax.broadcasted_iota(jnp.int32, (BLOCK, BLOCK), 1)
    ).astype(F32)
    total = jnp.zeros((heads, 1), F32)
    for b in range(blocks):
        at = slice(b * BLOCK, (b + 1) * BLOCK)
        c = lax.dot_general(
            logrows[:, at], upper, (((1,), (0,)), ((), ())),
            precision=lax.Precision.HIGHEST, preferred_element_type=F32,
        )
        last = c[:, BLOCK - 1 :]
        crow[:, at] = c * LOG2E
        erow[:, at] = jnp.exp(c)
        krow[:, at] = jnp.exp(last - c)
        total = total + last
        dblock[b] = jnp.exp(jnp.broadcast_to(last, (heads, HEAD_DIM)))
    decay = jnp.exp(jnp.broadcast_to(total, (heads, HEAD_DIM)))
    for h in range(heads):
        dec[h] = decay[h : h + 1, :]

    @pl.when(is_first)
    def _():
        before[...] = jnp.zeros_like(before)

        @pl.when(r == 0)
        def _():
            prior[1] = jnp.zeros(prior.shape[1:], F32)

    pl.semaphore_wait(barrier, n + peers - 2)
    send_dec().start()

    def make_local(i, carry):
        load(0, i).wait()
        load(1, i).wait()
        for e in range(group):
            h = i * group + e
            row = krow[pl.ds(h, 1), :]
            state = None
            for b in range(blocks):
                at = slice(b * BLOCK, (b + 1) * BLOCK)
                kt = ks[i, at, e * HEAD_DIM : (e + 1) * HEAD_DIM].astype(F32).T
                pair = jnp.dot(
                    split(kt * row[:, at], 0), vs[i, at, e * HEAD_DIM : (e + 1) * HEAD_DIM],
                    preferred_element_type=F32,
                )
                fresh = pair[:HEAD_DIM] + pair[HEAD_DIM:]
                state = fresh if b == 0 else dblock[b, pl.ds(h, 1), :] * state + fresh
                if b < blocks - 1:
                    first[b, h] = state
            local[0, h], local[1, h] = halves(state)
        send_local(i).start()
        return carry

    lax.fori_loop(0, chunks, make_local, 0)
    send_dec().wait_recv()

    def chain(i):
        send_local(i).wait_recv()

        @pl.when(jnp.logical_not(is_first))
        def _():
            send_after(i).wait_recv()

        at = span(i)
        mine, their = local[r, at], theirs[at]
        d_mine, d_their = dec[at], dec_theirs[at]
        came = before[at]
        even = r == 0
        grown = d_mine * d_their * came + jnp.where(
            even, d_their * mine + their, d_mine * their + mine
        )
        after[at] = grown

        @pl.when(jnp.logical_not(is_last))
        def _():
            send_after(i).start()

        prior[r, at] = jnp.where(even, came, d_their * came + their)

        give[at] = jnp.where(even, d_mine * came + mine, came)

        @pl.when(jnp.logical_not(is_first & (r == 1)))
        def _():
            send_prior(i).start()

        @pl.when(is_last)
        def _():
            for s in range(groups):
                fsend[s, at] = grown[:, s * rows : (s + 1) * rows, :]

            def give_final(s, carry):
                @pl.when(owner(s) != me)
                def _():
                    send_final(i, s).start()

                @pl.when(owner(s) == me)
                def _():
                    frecv[at] = fsend[s, at]

                return carry

            lax.fori_loop(0, groups, give_final, 0)

    side = BLOCK // 2
    lower = lax.broadcasted_iota(jnp.int32, (side, side), 0) >= lax.broadcasted_iota(
        jnp.int32, (side, side), 1
    )

    def intra(i):
        load(2, i).wait()
        for e in range(group):
            h = i * group + e
            cut = slice(e * HEAD_DIM, (e + 1) * HEAD_DIM)
            row = crow[pl.ds(h, 1), :]
            column = jnp.broadcast_to(row, (side, tokens)).T
            for b in range(blocks):
                at = slice(b * BLOCK, (b + 1) * BLOCK)
                scores = lax.dot_general(
                    qs[i, at, cut], ks[i, at, cut], (((1,), (1,)), ((), ())),
                    preferred_element_type=F32,
                )

                def weights(t, s):
                    rise = column[b * BLOCK + t : b * BLOCK + t + side, :] - (
                        row[:, b * BLOCK + s : b * BLOCK + s + side]
                    )
                    factor = jnp.exp2(rise)
                    if t == s:
                        factor = jnp.where(lower, factor, 0.0)
                    return (scores[t : t + side, s : s + side] * factor).astype(BF16)

                acc[h, b * BLOCK : b * BLOCK + side, :] = jnp.dot(
                    weights(0, 0), vs[i, b * BLOCK : b * BLOCK + side, cut],
                    preferred_element_type=F32,
                )
                acc[h, b * BLOCK + side : (b + 1) * BLOCK, :] = jnp.dot(
                    jnp.concatenate([weights(side, 0), weights(side, side)], axis=1),
                    vs[i, at, cut], preferred_element_type=F32,
                )

    lag = jnp.minimum(g, chunks)

    def middle(j, carry):
        @pl.when((j >= lag) & (j - lag < chunks))
        def _():
            chain(j - lag)

        @pl.when(j < chunks)
        def _():
            intra(j)

        return carry

    lax.fori_loop(0, chunks + min(groups - 1, chunks), middle, 0)

    def carried(i, sums):
        @pl.when(jnp.logical_not(is_first & (r == 0)))
        def _():
            send_prior(i).wait_recv()

        for e in range(group):
            h = i * group + e
            cut = slice(e * HEAD_DIM, (e + 1) * HEAD_DIM)
            start = joined(prior[0, h], prior[1, h])
            grows = jnp.broadcast_to(erow[pl.ds(h, 1), :], (HEAD_DIM, tokens)).T
            decayed = None
            parts = []
            for b in range(blocks):
                at = slice(b * BLOCK, (b + 1) * BLOCK)
                if b == 0:
                    state = start
                else:
                    state = decayed * start + first[b - 1, h]
                grow = grows[at]
                last = dblock[b, pl.ds(h, 1), :]
                decayed = last if b == 0 else decayed * last
                qb = qs[i, at, cut]
                inter = jnp.dot(
                    jnp.concatenate([qb, qb], axis=1), split(state, 0),
                    preferred_element_type=F32,
                )
                out = acc[h, at, :] + grow * inter
                acc[h, at, :] = out
                parts.append(out * out)
            sums = sums + jnp.concatenate(parts, axis=0)
        return sums

    sums = lax.fori_loop(0, chunks, carried, jnp.zeros((tokens, HEAD_DIM), F32))
    squares[0] = jnp.sum(sums.T, axis=0, keepdims=True)
    for step in range(1, peers):
        send_squares(step).start()
    for step in range(1, peers):
        send_squares(step).wait_recv()
    whole = squares[0]
    for step in range(1, peers):
        whole = whole + squares[step]
    scale = lax.rsqrt(whole / D + EPS)
    scale = jnp.broadcast_to(scale, (HEAD_DIM, tokens)).T

    def finish(i, carry):
        for e in range(group):
            h = i * group + e
            gain = gain_ref[:, pl.ds(pl.multiple_of(h * HEAD_DIM, HEAD_DIM), HEAD_DIM)]
            outs[i, :, e * HEAD_DIM : (e + 1) * HEAD_DIM] = (acc[h] * scale * gain).astype(BF16)
        store(i).start()
        return carry

    lax.fori_loop(0, chunks, finish, 0)

    def drain(i, carry):
        send_local(i).wait_send()

        @pl.when(jnp.logical_not(is_last))
        def _():
            send_after(i).wait_send()

        @pl.when(jnp.logical_not(is_first & (r == 1)))
        def _():
            send_prior(i).wait_send()

        @pl.when(is_last)
        def _():
            def sent(s, carry):
                @pl.when(owner(s) != me)
                def _():
                    send_final(i, s).wait_send()

                return carry

            lax.fori_loop(0, groups, sent, 0)

        @pl.when(jnp.logical_not(is_last & ((me * rows // piece) % 2 == r)))
        def _():
            send_final(i, 0).wait_recv()

        store(i).wait()
        return carry

    lax.fori_loop(0, chunks, drain, 0)
    send_dec().wait_send()
    for step in range(1, peers):
        send_squares(step).wait_send()
    for at in range(rows):
        final_ref[:, at * HEAD_DIM : (at + 1) * HEAD_DIM] = frecv[:, at, :]


def on_device(n, peers, q, k, v, pace, surplus, gain):
    tokens, width = q.shape
    heads = pace.shape[0]
    group = 2
    chunks = heads // group
    blocks = tokens // BLOCK
    groups = n // 2
    rows = HEAD_DIM // n
    vmem = pltpu.VMEM
    dma = pltpu.SemaphoreType.DMA
    half = (heads, HALF, HEAD_DIM)
    flops = 2 * heads * tokens * HEAD_DIM * (2 * BLOCK + 4 * HEAD_DIM)
    return pl.pallas_call(
        functools.partial(kernel, n, peers, heads, group),
        out_shape=(
            jax.ShapeDtypeStruct((tokens, width), BF16),
            jax.ShapeDtypeStruct((heads, rows * HEAD_DIM), F32),
        ),
        in_specs=[pl.BlockSpec(memory_space=pl.ANY)] * 3
        + [pl.BlockSpec(memory_space=pltpu.VMEM)] * 3,
        out_specs=(
            pl.BlockSpec(memory_space=pl.ANY),
            pl.BlockSpec(memory_space=pltpu.VMEM),
        ),
        scratch_shapes=[
            vmem((chunks, tokens, group * HEAD_DIM), BF16),
            vmem((chunks, tokens, group * HEAD_DIM), BF16),
            vmem((chunks, tokens, group * HEAD_DIM), BF16),
            vmem((chunks, tokens, group * HEAD_DIM), BF16),
            vmem((heads, tokens, HEAD_DIM), F32),
            vmem((heads, tokens), F32),
            vmem((heads, tokens), F32),
            vmem((heads, tokens), F32),
            vmem((blocks, heads, HEAD_DIM), F32),
            vmem((max(blocks - 1, 1), heads, HEAD_DIM, HEAD_DIM), F32),
            vmem((2,) + half, F32),
            vmem(half, F32),
            vmem((2,) + half, F32),
            vmem(half, F32),
            vmem(half, F32),
            vmem(half, F32),
            vmem((heads, 1, HEAD_DIM), F32),
            vmem((heads, 1, HEAD_DIM), F32),
            vmem((groups, heads, rows, HEAD_DIM), F32),
            vmem((heads, rows, HEAD_DIM), F32),
            vmem((peers, 1, tokens), F32),
            dma((3, chunks)),
            dma((chunks,)),
            dma((2,)),
            dma((chunks,)),
            dma((chunks,)),
            dma((chunks,)),
            dma((chunks,)),
            dma((chunks,)),
            dma((chunks,)),
            dma((chunks, groups)),
            dma((chunks,)),
            dma((peers,)),
            dma((peers,)),
        ],
        compiler_params=pltpu.CompilerParams(
            collective_id=0, has_side_effects=True, vmem_limit_bytes=56 * 1024 * 1024
        ),
        cost_estimate=pl.CostEstimate(
            flops=flops, bytes_accessed=8 * tokens * width, transcendentals=heads * tokens * BLOCK
        ),
        name="chained_attention",
    )(q, k, v, pace.reshape(1, heads), surplus.T, gain.reshape(1, width))


def solution(mesh):
    in_specs = (P("seq", "tp"), P("seq", "tp"), P("seq", "tp"), P("tp"), P("seq", "tp"), P("tp"))
    out_specs = (P("seq", "tp"), P("tp", "seq"))
    return jax.shard_map(
        functools.partial(on_device, mesh.shape["seq"], mesh.shape["tp"]),
        mesh=mesh, in_specs=in_specs, out_specs=out_specs, check_vma=False,
    )
```

```python
import functools

import jax
import jax.numpy as jnp
from jax import lax
from jax.experimental import pallas as pl
from jax.experimental.pallas import tpu as pltpu
from jax.sharding import PartitionSpec as P

HEAD_DIM = 128
HALF = HEAD_DIM // 2
BLOCK = 256
D = 8192
EPS = 1e-06
LOG2E = 1.4426950408889634
F32 = jnp.float32
BF16 = jnp.bfloat16
MESH = pl.DeviceIdType.MESH


def split(x, axis):
    high = x.astype(BF16)
    low = (x - high.astype(F32)).astype(BF16)
    return jnp.concatenate([high, low], axis=axis)


def kernel(
    n, peers, heads, group,
    q_hbm, k_hbm, v_hbm, pace_ref, surplus_ref,
    acc, scale_ref, final_ref,
    qs, ks, vs, crow, erow, krow, dblock, first, local, theirs, prior, before, after, give,
    dec, dec_theirs, fsend, frecv, squares,
    load_sem, dec_sem, l_send, l_recv, p_send, p_recv, x_send, x_recv,
    f_send, f_recv, s_send, s_recv,
):
    tokens = q_hbm.shape[0]
    blocks = tokens // BLOCK
    chunks = heads // group
    wide = group * HEAD_DIM
    groups = n // 2
    rows = HEAD_DIM // n
    piece = max(rows, 8)
    me = lax.axis_index("seq")
    place = lax.axis_index("tp")
    g, r = me // 2, me % 2
    other = 1 - r
    partner = 2 * g + other

    def owner(s):
        top = s * rows
        return ((top // piece) * 2 * piece + r * piece + top % piece) // rows

    def halves(x):
        return [
            jnp.concatenate(
                [x[at : at + piece] for at in range(p * piece, HEAD_DIM, 2 * piece)], axis=0
            )
            for p in range(2)
        ]

    def joined(a, b):
        return jnp.concatenate(
            [x[at : at + piece] for at in range(0, HALF, piece) for x in (a, b)], axis=0
        )

    is_first, is_last = g == 0, g == groups - 1

    barrier = pltpu.get_barrier_semaphore()
    for step in range(1, n):
        pl.semaphore_signal(
            barrier, inc=1, device_id={"seq": lax.rem(me + step, n)}, device_id_type=MESH
        )
    for step in range(1, peers):
        pl.semaphore_signal(
            barrier, inc=1, device_id={"tp": lax.rem(place + step, peers)}, device_id_type=MESH
        )

    def lanes(i):
        return pl.ds(pl.multiple_of(i * wide, wide), wide)

    def load(which, i):
        source = (k_hbm, v_hbm, q_hbm)[which]
        target = (ks, vs, qs)[which]
        return pltpu.make_async_copy(
            source.at[:, lanes(i)], target.at[i], load_sem.at[which, i]
        )

    def span(i):
        return pl.ds(i * group, group)

    def send_dec():
        return pltpu.make_async_remote_copy(
            src_ref=dec, dst_ref=dec_theirs, send_sem=dec_sem.at[0], recv_sem=dec_sem.at[1],
            device_id={"seq": partner}, device_id_type=MESH,
        )

    def send_local(i):
        return pltpu.make_async_remote_copy(
            src_ref=local.at[other, span(i)], dst_ref=theirs.at[span(i)],
            send_sem=l_send.at[i], recv_sem=l_recv.at[i],
            device_id={"seq": partner}, device_id_type=MESH,
        )

    def send_after(i):
        return pltpu.make_async_remote_copy(
            src_ref=after.at[span(i)], dst_ref=before.at[span(i)],
            send_sem=p_send.at[i], recv_sem=p_recv.at[i],
            device_id={"seq": lax.rem(me + 2, n)}, device_id_type=MESH,
        )

    def send_prior(i):
        return pltpu.make_async_remote_copy(
            src_ref=give.at[span(i)], dst_ref=prior.at[r, span(i)],
            send_sem=x_send.at[i], recv_sem=x_recv.at[i],
            device_id={"seq": partner}, device_id_type=MESH,
        )

    def send_final(i, s):
        return pltpu.make_async_remote_copy(
            src_ref=fsend.at[s, span(i)], dst_ref=frecv.at[span(i)],
            send_sem=f_send.at[i, s], recv_sem=f_recv.at[i],
            device_id={"seq": owner(s)}, device_id_type=MESH,
        )

    def send_squares(step):
        return pltpu.make_async_remote_copy(
            src_ref=squares.at[0], dst_ref=squares.at[step],
            send_sem=s_send.at[step], recv_sem=s_recv.at[step],
            device_id={"tp": lax.rem(place + step, peers)}, device_id_type=MESH,
        )

    for i in range(chunks):
        load(0, i).start()
        load(1, i).start()

    square = (heads, heads)
    diagonal = lax.broadcasted_iota(jnp.int32, square, 0) == lax.broadcasted_iota(
        jnp.int32, square, 1
    )
    pace = jnp.sum(
        jnp.where(diagonal, jnp.broadcast_to(pace_ref[...], square), 0.0), axis=1, keepdims=True
    )
    logrows = surplus_ref[...] - pace
    upper = (
        lax.broadcasted_iota(jnp.int32, (BLOCK, BLOCK), 0)
        <= lax.broadcasted_iota(jnp.int32, (BLOCK, BLOCK), 1)
    ).astype(F32)
    total = jnp.zeros((heads, 1), F32)
    for b in range(blocks):
        at = slice(b * BLOCK, (b + 1) * BLOCK)
        c = lax.dot_general(
            logrows[:, at], upper, (((1,), (0,)), ((), ())),
            precision=lax.Precision.HIGHEST, preferred_element_type=F32,
        )
        last = c[:, BLOCK - 1 :]
        crow[:, at] = c * LOG2E
        erow[:, at] = jnp.exp(c)
        krow[:, at] = jnp.exp(last - c)
        total = total + last
        dblock[b] = jnp.exp(jnp.broadcast_to(last, (heads, HEAD_DIM)))
    decay = jnp.exp(jnp.broadcast_to(total, (heads, HEAD_DIM)))
    for h in range(heads):
        dec[h] = decay[h : h + 1, :]

    @pl.when(is_first)
    def _():
        before[...] = jnp.zeros_like(before)

        @pl.when(r == 0)
        def _():
            prior[1] = jnp.zeros(prior.shape[1:], F32)

    pl.semaphore_wait(barrier, n + peers - 2)
    send_dec().start()

    def make_local(pair, carry):
        for e in range(2):
            h = pair * 2 + e
            load(0, h).wait()
            load(1, h).wait()
            load(2, h).start()
        for e in range(2):
            h = pair * 2 + e
            row = krow[pl.ds(h, 1), :]
            state = None
            for b in range(blocks):
                at = slice(b * BLOCK, (b + 1) * BLOCK)
                kt = ks[h, at, :].astype(F32).T
                both = jnp.dot(
                    split(kt * row[:, at], 0), vs[h, at, :], preferred_element_type=F32
                )
                fresh = both[:HEAD_DIM] + both[HEAD_DIM:]
                state = fresh if b == 0 else dblock[b, pl.ds(h, 1), :] * state + fresh
                if b < blocks - 1:
                    first[b, h] = state
            local[0, h], local[1, h] = halves(state)
        for e in range(2):
            send_local(pair * 2 + e).start()
        return carry

    lax.fori_loop(0, heads // 2, make_local, 0)
    send_dec().wait_recv()

    hold = jnp.maximum(chunks // 2 - 2 * g, 0)

    def chain(i):
        send_local(i).wait_recv()

        @pl.when(jnp.logical_not(is_first))
        def _():
            send_after(i).wait_recv()

        at = span(i)
        mine, their = local[r, at], theirs[at]
        d_mine, d_their = dec[at], dec_theirs[at]
        came = before[at]
        even = r == 0
        grown = d_mine * d_their * came + jnp.where(
            even, d_their * mine + their, d_mine * their + mine
        )
        after[at] = grown

        @pl.when(jnp.logical_not(is_last))
        def _():
            send_after(i).start()

        prior[r, at] = jnp.where(even, came, d_their * came + their)

        give[at] = jnp.where(even, d_mine * came + mine, came)

        @pl.when(jnp.logical_not(is_first & (r == 1)))
        def _():
            @pl.when(i >= hold)
            def _():
                send_prior(i - hold).start()

            @pl.when(i == chunks - 1)
            def _():
                def rest(t, carry):
                    @pl.when(t >= chunks - hold)
                    def _():
                        send_prior(t).start()

                    return carry

                lax.fori_loop(0, chunks, rest, 0)

        @pl.when(is_last)
        def _():
            for s in range(groups):
                fsend[s, at] = grown[:, s * rows : (s + 1) * rows, :]

            def give_final(s, carry):
                @pl.when(owner(s) != me)
                def _():
                    send_final(i, s).start()

                @pl.when(owner(s) == me)
                def _():
                    frecv[at] = fsend[s, at]

                return carry

            lax.fori_loop(0, groups, give_final, 0)

    side = BLOCK // 2
    lower = lax.broadcasted_iota(jnp.int32, (side, side), 0) >= lax.broadcasted_iota(
        jnp.int32, (side, side), 1
    )

    def intra(i):
        load(2, i).wait()
        for e in range(group):
            h = i * group + e
            cut = slice(e * HEAD_DIM, (e + 1) * HEAD_DIM)
            row = crow[pl.ds(h, 1), :]
            column = jnp.broadcast_to(row, (side, tokens)).T
            for b in range(blocks):
                at = slice(b * BLOCK, (b + 1) * BLOCK)
                scores = lax.dot_general(
                    qs[i, at, cut], ks[i, at, cut], (((1,), (1,)), ((), ())),
                    preferred_element_type=F32,
                )

                def weights(t, s):
                    rise = column[b * BLOCK + t : b * BLOCK + t + side, :] - (
                        row[:, b * BLOCK + s : b * BLOCK + s + side]
                    )
                    factor = jnp.exp2(rise)
                    if t == s:
                        factor = jnp.where(lower, factor, 0.0)
                    return (scores[t : t + side, s : s + side] * factor).astype(BF16)

                acc[h, b * BLOCK : b * BLOCK + side, :] = jnp.dot(
                    weights(0, 0), vs[i, b * BLOCK : b * BLOCK + side, cut],
                    preferred_element_type=F32,
                )
                acc[h, b * BLOCK + side : (b + 1) * BLOCK, :] = jnp.dot(
                    jnp.concatenate([weights(side, 0), weights(side, side)], axis=1),
                    vs[i, at, cut], preferred_element_type=F32,
                )

    lag = jnp.minimum(3 * g, chunks)

    def middle(j, carry):
        @pl.when((j >= lag) & (j - lag < chunks))
        def _():
            chain(j - lag)

        @pl.when(j < chunks)
        def _():
            intra(j)

        return carry

    lax.fori_loop(0, chunks + min(3 * (groups - 1), chunks), middle, 0)

    def carried(i, sums):
        @pl.when(jnp.logical_not(is_first & (r == 0)))
        def _():
            send_prior(i).wait_recv()

        for e in range(group):
            h = i * group + e
            cut = slice(e * HEAD_DIM, (e + 1) * HEAD_DIM)
            start = joined(prior[0, h], prior[1, h])
            grows = jnp.broadcast_to(erow[pl.ds(h, 1), :], (HEAD_DIM, tokens)).T
            decayed = None
            parts = []
            for b in range(blocks):
                at = slice(b * BLOCK, (b + 1) * BLOCK)
                if b == 0:
                    state = start
                else:
                    state = decayed * start + first[b - 1, h]
                grow = grows[at]
                last = dblock[b, pl.ds(h, 1), :]
                decayed = last if b == 0 else decayed * last
                qb = qs[i, at, cut]
                inter = jnp.dot(
                    jnp.concatenate([qb, qb], axis=1), split(state, 0),
                    preferred_element_type=F32,
                )
                out = acc[h, at, :] + grow * inter
                acc[h, at, :] = out
                parts.append(out * out)
            sums = sums + jnp.concatenate(parts, axis=0)
        return sums

    sums = lax.fori_loop(0, chunks, carried, jnp.zeros((tokens, HEAD_DIM), F32))
    squares[0] = jnp.sum(sums.T, axis=0, keepdims=True)
    for step in range(1, peers):
        send_squares(step).start()
    for step in range(1, peers):
        send_squares(step).wait_recv()
    whole = squares[0]
    for step in range(1, peers):
        whole = whole + squares[step]
    scale = lax.rsqrt(whole / D + EPS)
    scale_ref[...] = scale

    def drain(i, carry):
        send_local(i).wait_send()

        @pl.when(jnp.logical_not(is_last))
        def _():
            send_after(i).wait_send()

        @pl.when(jnp.logical_not(is_first & (r == 1)))
        def _():
            send_prior(i).wait_send()

        @pl.when(is_last)
        def _():
            def sent(s, carry):
                @pl.when(owner(s) != me)
                def _():
                    send_final(i, s).wait_send()

                return carry

            lax.fori_loop(0, groups, sent, 0)

        @pl.when(jnp.logical_not(is_last & ((me * rows // piece) % 2 == r)))
        def _():
            send_final(i, 0).wait_recv()

        return carry

    lax.fori_loop(0, chunks, drain, 0)
    send_dec().wait_send()
    for step in range(1, peers):
        send_squares(step).wait_send()
    final_ref[...] = frecv[...]


def norm_kernel(acc, scale_ref, gain_ref, final_in, out_hbm, final_ref, outs, store_sem):
    heads, tokens = acc.shape[:2]
    rows = final_in.shape[1]
    wide = outs.shape[2]
    group = wide // HEAD_DIM
    scale = jnp.broadcast_to(scale_ref[...], (HEAD_DIM, tokens)).T

    def store(i):
        return pltpu.make_async_copy(
            outs.at[i], out_hbm.at[:, pl.ds(pl.multiple_of(i * wide, wide), wide)], store_sem.at[i]
        )

    def finish(i, carry):
        for e in range(group):
            h = i * group + e
            gain = gain_ref[:, pl.ds(pl.multiple_of(h * HEAD_DIM, HEAD_DIM), HEAD_DIM)]
            outs[i, :, e * HEAD_DIM : (e + 1) * HEAD_DIM] = (acc[h] * scale * gain).astype(BF16)
        store(i).start()
        return carry

    lax.fori_loop(0, heads // group, finish, 0)
    for at in range(rows):
        final_ref[:, at * HEAD_DIM : (at + 1) * HEAD_DIM] = final_in[:, at, :]

    def drain(i, carry):
        store(i).wait()
        return carry

    lax.fori_loop(0, heads // group, drain, 0)


def on_device(n, peers, q, k, v, pace, surplus, gain):
    tokens, width = q.shape
    heads = pace.shape[0]
    group = 1
    chunks = heads // group
    blocks = tokens // BLOCK
    groups = n // 2
    rows = HEAD_DIM // n
    vmem = pltpu.VMEM
    dma = pltpu.SemaphoreType.DMA
    half = (heads, HALF, HEAD_DIM)
    flops = 2 * heads * tokens * HEAD_DIM * (2 * BLOCK + 4 * HEAD_DIM)
    acc, scale, final = pl.pallas_call(
        functools.partial(kernel, n, peers, heads, group),
        out_shape=(
            vmem((heads, tokens, HEAD_DIM), F32),
            vmem((1, tokens), F32),
            vmem((heads, rows, HEAD_DIM), F32),
        ),
        in_specs=[pl.BlockSpec(memory_space=pl.ANY)] * 3
        + [pl.BlockSpec(memory_space=pltpu.VMEM)] * 2,
        out_specs=[pl.BlockSpec(memory_space=pltpu.VMEM)] * 3,
        scratch_shapes=[
            vmem((chunks, tokens, group * HEAD_DIM), BF16),
            vmem((chunks, tokens, group * HEAD_DIM), BF16),
            vmem((chunks, tokens, group * HEAD_DIM), BF16),
            vmem((heads, tokens), F32),
            vmem((heads, tokens), F32),
            vmem((heads, tokens), F32),
            vmem((blocks, heads, HEAD_DIM), F32),
            vmem((max(blocks - 1, 1), heads, HEAD_DIM, HEAD_DIM), F32),
            vmem((2,) + half, F32),
            vmem(half, F32),
            vmem((2,) + half, F32),
            vmem(half, F32),
            vmem(half, F32),
            vmem(half, F32),
            vmem((heads, 1, HEAD_DIM), F32),
            vmem((heads, 1, HEAD_DIM), F32),
            vmem((groups, heads, rows, HEAD_DIM), F32),
            vmem((heads, rows, HEAD_DIM), F32),
            vmem((peers, 1, tokens), F32),
            dma((3, chunks)),
            dma((2,)),
            dma((chunks,)),
            dma((chunks,)),
            dma((chunks,)),
            dma((chunks,)),
            dma((chunks,)),
            dma((chunks,)),
            dma((chunks, groups)),
            dma((chunks,)),
            dma((peers,)),
            dma((peers,)),
        ],
        compiler_params=pltpu.CompilerParams(
            collective_id=0, has_side_effects=True, vmem_limit_bytes=58 * 1024 * 1024
        ),
        cost_estimate=pl.CostEstimate(
            flops=flops, bytes_accessed=8 * tokens * width, transcendentals=heads * tokens * BLOCK
        ),
        name="chained_attention",
    )(q, k, v, pace.reshape(1, heads), surplus.T)
    return pl.pallas_call(
        norm_kernel,
        out_shape=(
            jax.ShapeDtypeStruct((tokens, width), BF16),
            jax.ShapeDtypeStruct((heads, rows * HEAD_DIM), F32),
        ),
        in_specs=[pl.BlockSpec(memory_space=pltpu.VMEM)] * 4,
        out_specs=(
            pl.BlockSpec(memory_space=pl.ANY),
            pl.BlockSpec(memory_space=pltpu.VMEM),
        ),
        scratch_shapes=[vmem((heads // 2, tokens, 2 * HEAD_DIM), BF16), dma((heads // 2,))],
        compiler_params=pltpu.CompilerParams(vmem_limit_bytes=16 * 1024 * 1024),
        cost_estimate=pl.CostEstimate(
            flops=3 * tokens * width, bytes_accessed=6 * tokens * width, transcendentals=0
        ),
        name="norm",
    )(acc, scale, gain.reshape(1, width), final)


def solution(mesh):
    in_specs = (P("seq", "tp"), P("seq", "tp"), P("seq", "tp"), P("tp"), P("seq", "tp"), P("tp"))
    out_specs = (P("seq", "tp"), P("tp", "seq"))
    return jax.shard_map(
        functools.partial(on_device, mesh.shape["seq"], mesh.shape["tp"]),
        mesh=mesh, in_specs=in_specs, out_specs=out_specs, check_vma=False,
    )
```

```python
import functools

import jax
import jax.numpy as jnp
from jax import lax
from jax.experimental import pallas as pl
from jax.experimental.pallas import tpu as pltpu
from jax.sharding import PartitionSpec as P

HEAD_DIM = 128
HALF = HEAD_DIM // 2
BLOCK = 256
D = 8192
EPS = 1e-06
LOG2E = 1.4426950408889634
F32 = jnp.float32
BF16 = jnp.bfloat16
MESH = pl.DeviceIdType.MESH


def split(x, axis):
    high = x.astype(BF16)
    low = (x - high.astype(F32)).astype(BF16)
    return jnp.concatenate([high, low], axis=axis)


def kernel(
    n, peers, heads, group,
    q_hbm, k_hbm, v_hbm, pace_ref, surplus_ref,
    acc, scale_ref, final_ref,
    qs, ks, vs, crow, erow, krow, dblock, first, local, theirs, prior, before, after, give,
    dec, dec_theirs, fsend, frecv, squares,
    load_sem, dec_sem, l_send, l_recv, p_send, p_recv, x_send, x_recv,
    f_send, f_recv, s_send, s_recv,
):
    tokens = q_hbm.shape[0]
    blocks = tokens // BLOCK
    chunks = heads // group
    wide = group * HEAD_DIM
    groups = n // 2
    rows = HEAD_DIM // n
    piece = max(rows, 8)
    me = lax.axis_index("seq")
    place = lax.axis_index("tp")
    g, r = me // 2, me % 2
    other = 1 - r
    partner = 2 * g + other

    def owner(s):
        top = s * rows
        return ((top // piece) * 2 * piece + r * piece + top % piece) // rows

    def halves(x):
        return [
            jnp.concatenate(
                [x[at : at + piece] for at in range(p * piece, HEAD_DIM, 2 * piece)], axis=0
            )
            for p in range(2)
        ]

    def joined(a, b):
        return jnp.concatenate(
            [x[at : at + piece] for at in range(0, HALF, piece) for x in (a, b)], axis=0
        )

    is_first, is_last = g == 0, g == groups - 1

    barrier = pltpu.get_barrier_semaphore()
    for step in range(1, n):
        pl.semaphore_signal(
            barrier, inc=1, device_id={"seq": lax.rem(me + step, n)}, device_id_type=MESH
        )
    for step in range(1, peers):
        pl.semaphore_signal(
            barrier, inc=1, device_id={"tp": lax.rem(place + step, peers)}, device_id_type=MESH
        )

    def lanes(i):
        return pl.ds(pl.multiple_of(i * wide, wide), wide)

    def load(which, i):
        source = (k_hbm, v_hbm, q_hbm)[which]
        target = (ks, vs, qs)[which]
        return pltpu.make_async_copy(
            source.at[:, lanes(i)], target.at[i], load_sem.at[which, i]
        )

    def span(i):
        return pl.ds(i * group, group)

    def send_dec():
        return pltpu.make_async_remote_copy(
            src_ref=dec, dst_ref=dec_theirs, send_sem=dec_sem.at[0], recv_sem=dec_sem.at[1],
            device_id={"seq": partner}, device_id_type=MESH,
        )

    def send_local(i):
        return pltpu.make_async_remote_copy(
            src_ref=local.at[other, span(i)], dst_ref=theirs.at[span(i)],
            send_sem=l_send.at[i], recv_sem=l_recv.at[i],
            device_id={"seq": partner}, device_id_type=MESH,
        )

    def send_after(i):
        return pltpu.make_async_remote_copy(
            src_ref=after.at[span(i)], dst_ref=before.at[span(i)],
            send_sem=p_send.at[i], recv_sem=p_recv.at[i],
            device_id={"seq": lax.rem(me + 2, n)}, device_id_type=MESH,
        )

    def send_prior(i):
        return pltpu.make_async_remote_copy(
            src_ref=give.at[span(i)], dst_ref=prior.at[r, span(i)],
            send_sem=x_send.at[i], recv_sem=x_recv.at[i],
            device_id={"seq": partner}, device_id_type=MESH,
        )

    def send_final(i, s):
        return pltpu.make_async_remote_copy(
            src_ref=fsend.at[s, span(i)], dst_ref=frecv.at[span(i)],
            send_sem=f_send.at[i, s], recv_sem=f_recv.at[i],
            device_id={"seq": owner(s)}, device_id_type=MESH,
        )

    def send_squares(step):
        return pltpu.make_async_remote_copy(
            src_ref=squares.at[0], dst_ref=squares.at[step],
            send_sem=s_send.at[step], recv_sem=s_recv.at[step],
            device_id={"tp": lax.rem(place + step, peers)}, device_id_type=MESH,
        )

    for i in range(chunks):
        load(0, i).start()
        load(1, i).start()

    square = (heads, heads)
    diagonal = lax.broadcasted_iota(jnp.int32, square, 0) == lax.broadcasted_iota(
        jnp.int32, square, 1
    )
    pace = jnp.sum(
        jnp.where(diagonal, jnp.broadcast_to(pace_ref[...], square), 0.0), axis=1, keepdims=True
    )
    logrows = surplus_ref[...] - pace
    upper = (
        lax.broadcasted_iota(jnp.int32, (BLOCK, BLOCK), 0)
        <= lax.broadcasted_iota(jnp.int32, (BLOCK, BLOCK), 1)
    ).astype(F32)
    total = jnp.zeros((heads, 1), F32)
    for b in range(blocks):
        at = slice(b * BLOCK, (b + 1) * BLOCK)
        c = lax.dot_general(
            logrows[:, at], upper, (((1,), (0,)), ((), ())),
            precision=lax.Precision.HIGHEST, preferred_element_type=F32,
        )
        last = c[:, BLOCK - 1 :]
        crow[:, at] = c * LOG2E
        erow[:, at] = jnp.exp(c)
        krow[:, at] = jnp.exp(last - c)
        total = total + last
        dblock[b] = jnp.exp(jnp.broadcast_to(last, (heads, HEAD_DIM)))
    decay = jnp.exp(jnp.broadcast_to(total, (heads, HEAD_DIM)))
    for h in range(heads):
        dec[h] = decay[h : h + 1, :]

    @pl.when(is_first)
    def _():
        before[...] = jnp.zeros_like(before)

        @pl.when(r == 0)
        def _():
            prior[1] = jnp.zeros(prior.shape[1:], F32)

    pl.semaphore_wait(barrier, n + peers - 2)
    send_dec().start()

    def make_local(lump, carry):
        for e in range(4):
            h = lump * 4 + e
            load(0, h).wait()
            load(1, h).wait()
            load(2, h).start()
        for e in range(4):
            h = lump * 4 + e
            row = krow[pl.ds(h, 1), :]
            state = None
            for b in range(blocks):
                at = slice(b * BLOCK, (b + 1) * BLOCK)
                kt = ks[h, at, :].astype(F32).T
                both = jnp.dot(
                    split(kt * row[:, at], 0), vs[h, at, :], preferred_element_type=F32
                )
                fresh = both[:HEAD_DIM] + both[HEAD_DIM:]
                state = fresh if b == 0 else dblock[b, pl.ds(h, 1), :] * state + fresh
                if b < blocks - 1:
                    first[b, h] = state
            local[0, h], local[1, h] = halves(state)
        for e in range(4):
            send_local(lump * 4 + e).start()
        return carry

    lax.fori_loop(0, heads // 4, make_local, 0)
    send_dec().wait_recv()

    hold = jnp.maximum(chunks // 2 - 3 * g, 0)

    def chain(i):
        send_local(i).wait_recv()

        @pl.when(jnp.logical_not(is_first))
        def _():
            send_after(i).wait_recv()

        at = span(i)
        mine, their = local[r, at], theirs[at]
        d_mine, d_their = dec[at], dec_theirs[at]
        came = before[at]
        even = r == 0
        grown = d_mine * d_their * came + jnp.where(
            even, d_their * mine + their, d_mine * their + mine
        )
        after[at] = grown

        @pl.when(jnp.logical_not(is_last))
        def _():
            send_after(i).start()

        prior[r, at] = jnp.where(even, came, d_their * came + their)

        give[at] = jnp.where(even, d_mine * came + mine, came)

        @pl.when(jnp.logical_not(is_first & (r == 1)))
        def _():
            @pl.when(i >= hold)
            def _():
                send_prior(i - hold).start()

            @pl.when(i == chunks - 1)
            def _():
                def rest(t, carry):
                    @pl.when(t >= chunks - hold)
                    def _():
                        send_prior(t).start()

                    return carry

                lax.fori_loop(0, chunks, rest, 0)

        @pl.when(is_last)
        def _():
            for s in range(groups):
                fsend[s, at] = grown[:, s * rows : (s + 1) * rows, :]

            def give_final(s, carry):
                @pl.when(owner(s) != me)
                def _():
                    send_final(i, s).start()

                @pl.when(owner(s) == me)
                def _():
                    frecv[at] = fsend[s, at]

                return carry

            lax.fori_loop(0, groups, give_final, 0)

    side = BLOCK // 2
    lower = lax.broadcasted_iota(jnp.int32, (side, side), 0) >= lax.broadcasted_iota(
        jnp.int32, (side, side), 1
    )

    def intra(i):
        for e in range(2):
            load(2, i * 2 + e).wait()
        for e in range(2):
            h = i * 2 + e
            row = crow[pl.ds(h, 1), :]
            column = jnp.broadcast_to(row, (side, tokens)).T
            for b in range(blocks):
                at = slice(b * BLOCK, (b + 1) * BLOCK)
                scores = lax.dot_general(
                    qs[h, at, :], ks[h, at, :], (((1,), (1,)), ((), ())),
                    preferred_element_type=F32,
                )

                def weights(t, s):
                    rise = column[b * BLOCK + t : b * BLOCK + t + side, :] - (
                        row[:, b * BLOCK + s : b * BLOCK + s + side]
                    )
                    factor = jnp.exp2(rise)
                    if t == s:
                        factor = jnp.where(lower, factor, 0.0)
                    return (scores[t : t + side, s : s + side] * factor).astype(BF16)

                acc[h, b * BLOCK : b * BLOCK + side, :] = jnp.dot(
                    weights(0, 0), vs[h, b * BLOCK : b * BLOCK + side, :],
                    preferred_element_type=F32,
                )
                acc[h, b * BLOCK + side : (b + 1) * BLOCK, :] = jnp.dot(
                    jnp.concatenate([weights(side, 0), weights(side, side)], axis=1),
                    vs[h, at, :], preferred_element_type=F32,
                )

    lumps = heads // 4
    lag = jnp.minimum(g, lumps)

    def middle(j, carry):
        @pl.when((j >= lag) & (j - lag < lumps))
        def _():
            def step(e, carry):
                chain((j - lag) * 4 + e)
                return carry

            lax.fori_loop(0, 4, step, 0)

        @pl.when(j < heads // 2)
        def _():
            intra(j)

        return carry

    lax.fori_loop(0, max(heads // 2, lumps + min(groups - 1, lumps)), middle, 0)

    def carried(i, sums):
        @pl.when(jnp.logical_not(is_first & (r == 0)))
        def _():
            for e in range(2):
                send_prior(i * 2 + e).wait_recv()

        for e in range(2):
            h = i * 2 + e
            start = joined(prior[0, h], prior[1, h])
            grows = jnp.broadcast_to(erow[pl.ds(h, 1), :], (HEAD_DIM, tokens)).T
            decayed = None
            parts = []
            for b in range(blocks):
                at = slice(b * BLOCK, (b + 1) * BLOCK)
                if b == 0:
                    state = start
                else:
                    state = decayed * start + first[b - 1, h]
                grow = grows[at]
                last = dblock[b, pl.ds(h, 1), :]
                decayed = last if b == 0 else decayed * last
                qb = qs[h, at, :]
                inter = jnp.dot(
                    jnp.concatenate([qb, qb], axis=1), split(state, 0),
                    preferred_element_type=F32,
                )
                out = acc[h, at, :] + grow * inter
                acc[h, at, :] = out
                parts.append(out * out)
            sums = sums + jnp.concatenate(parts, axis=0)
        return sums

    sums = lax.fori_loop(0, heads // 2, carried, jnp.zeros((tokens, HEAD_DIM), F32))
    squares[0] = jnp.sum(sums.T, axis=0, keepdims=True)
    for step in range(1, peers):
        send_squares(step).start()
    for step in range(1, peers):
        send_squares(step).wait_recv()
    whole = squares[0]
    for step in range(1, peers):
        whole = whole + squares[step]
    scale = lax.rsqrt(whole / D + EPS)
    scale_ref[...] = scale

    def drain(i, carry):
        send_local(i).wait_send()

        @pl.when(jnp.logical_not(is_last))
        def _():
            send_after(i).wait_send()

        @pl.when(jnp.logical_not(is_first & (r == 1)))
        def _():
            send_prior(i).wait_send()

        @pl.when(is_last)
        def _():
            def sent(s, carry):
                @pl.when(owner(s) != me)
                def _():
                    send_final(i, s).wait_send()

                return carry

            lax.fori_loop(0, groups, sent, 0)

        @pl.when(jnp.logical_not(is_last & ((me * rows // piece) % 2 == r)))
        def _():
            send_final(i, 0).wait_recv()

        return carry

    lax.fori_loop(0, chunks, drain, 0)
    send_dec().wait_send()
    for step in range(1, peers):
        send_squares(step).wait_send()
    final_ref[...] = frecv[...]


def norm_kernel(acc, scale_ref, gain_ref, final_in, out_hbm, final_ref, outs, store_sem):
    heads, tokens = acc.shape[:2]
    rows = final_in.shape[1]
    wide = outs.shape[2]
    group = wide // HEAD_DIM
    scale = jnp.broadcast_to(scale_ref[...], (HEAD_DIM, tokens)).T

    def store(i):
        return pltpu.make_async_copy(
            outs.at[i], out_hbm.at[:, pl.ds(pl.multiple_of(i * wide, wide), wide)], store_sem.at[i]
        )

    def finish(i, carry):
        for e in range(group):
            h = i * group + e
            gain = gain_ref[:, pl.ds(pl.multiple_of(h * HEAD_DIM, HEAD_DIM), HEAD_DIM)]
            outs[i, :, e * HEAD_DIM : (e + 1) * HEAD_DIM] = (acc[h] * scale * gain).astype(BF16)
        store(i).start()
        return carry

    lax.fori_loop(0, heads // group, finish, 0)
    for at in range(rows):
        final_ref[:, at * HEAD_DIM : (at + 1) * HEAD_DIM] = final_in[:, at, :]

    def drain(i, carry):
        store(i).wait()
        return carry

    lax.fori_loop(0, heads // group, drain, 0)


def on_device(n, peers, q, k, v, pace, surplus, gain):
    tokens, width = q.shape
    heads = pace.shape[0]
    group = 1
    chunks = heads // group
    blocks = tokens // BLOCK
    groups = n // 2
    rows = HEAD_DIM // n
    vmem = pltpu.VMEM
    dma = pltpu.SemaphoreType.DMA
    half = (heads, HALF, HEAD_DIM)
    flops = 2 * heads * tokens * HEAD_DIM * (2 * BLOCK + 4 * HEAD_DIM)
    acc, scale, final = pl.pallas_call(
        functools.partial(kernel, n, peers, heads, group),
        out_shape=(
            vmem((heads, tokens, HEAD_DIM), F32),
            vmem((1, tokens), F32),
            vmem((heads, rows, HEAD_DIM), F32),
        ),
        in_specs=[pl.BlockSpec(memory_space=pl.ANY)] * 3
        + [pl.BlockSpec(memory_space=pltpu.VMEM)] * 2,
        out_specs=[pl.BlockSpec(memory_space=pltpu.VMEM)] * 3,
        scratch_shapes=[
            vmem((chunks, tokens, group * HEAD_DIM), BF16),
            vmem((chunks, tokens, group * HEAD_DIM), BF16),
            vmem((chunks, tokens, group * HEAD_DIM), BF16),
            vmem((heads, tokens), F32),
            vmem((heads, tokens), F32),
            vmem((heads, tokens), F32),
            vmem((blocks, heads, HEAD_DIM), F32),
            vmem((max(blocks - 1, 1), heads, HEAD_DIM, HEAD_DIM), F32),
            vmem((2,) + half, F32),
            vmem(half, F32),
            vmem((2,) + half, F32),
            vmem(half, F32),
            vmem(half, F32),
            vmem(half, F32),
            vmem((heads, 1, HEAD_DIM), F32),
            vmem((heads, 1, HEAD_DIM), F32),
            vmem((groups, heads, rows, HEAD_DIM), F32),
            vmem((heads, rows, HEAD_DIM), F32),
            vmem((peers, 1, tokens), F32),
            dma((3, chunks)),
            dma((2,)),
            dma((chunks,)),
            dma((chunks,)),
            dma((chunks,)),
            dma((chunks,)),
            dma((chunks,)),
            dma((chunks,)),
            dma((chunks, groups)),
            dma((chunks,)),
            dma((peers,)),
            dma((peers,)),
        ],
        compiler_params=pltpu.CompilerParams(
            collective_id=0, has_side_effects=True, vmem_limit_bytes=58 * 1024 * 1024
        ),
        cost_estimate=pl.CostEstimate(
            flops=flops, bytes_accessed=8 * tokens * width, transcendentals=heads * tokens * BLOCK
        ),
        name="chained_attention",
    )(q, k, v, pace.reshape(1, heads), surplus.T)
    return pl.pallas_call(
        norm_kernel,
        out_shape=(
            jax.ShapeDtypeStruct((tokens, width), BF16),
            jax.ShapeDtypeStruct((heads, rows * HEAD_DIM), F32),
        ),
        in_specs=[pl.BlockSpec(memory_space=pltpu.VMEM)] * 4,
        out_specs=(
            pl.BlockSpec(memory_space=pl.ANY),
            pl.BlockSpec(memory_space=pltpu.VMEM),
        ),
        scratch_shapes=[vmem((heads // 2, tokens, 2 * HEAD_DIM), BF16), dma((heads // 2,))],
        compiler_params=pltpu.CompilerParams(vmem_limit_bytes=16 * 1024 * 1024),
        cost_estimate=pl.CostEstimate(
            flops=3 * tokens * width, bytes_accessed=6 * tokens * width, transcendentals=0
        ),
        name="norm",
    )(acc, scale, gain.reshape(1, width), final)


def solution(mesh):
    in_specs = (P("seq", "tp"), P("seq", "tp"), P("seq", "tp"), P("tp"), P("seq", "tp"), P("tp"))
    out_specs = (P("seq", "tp"), P("tp", "seq"))
    return jax.shard_map(
        functools.partial(on_device, mesh.shape["seq"], mesh.shape["tp"]),
        mesh=mesh, in_specs=in_specs, out_specs=out_specs, check_vma=False,
    )
```

```python
import functools

import jax
import jax.numpy as jnp
from jax import lax
from jax.experimental import pallas as pl
from jax.experimental.pallas import tpu as pltpu
from jax.sharding import PartitionSpec as P

HEAD_DIM = 128
HALF = HEAD_DIM // 2
BLOCK = 256
D = 8192
EPS = 1e-06
LOG2E = 1.4426950408889634
F32 = jnp.float32
BF16 = jnp.bfloat16
MESH = pl.DeviceIdType.MESH


def split(x, axis):
    high = x.astype(BF16)
    low = (x - high.astype(F32)).astype(BF16)
    return jnp.concatenate([high, low], axis=axis)


def kernel(
    n, peers, heads, group,
    q_hbm, k_hbm, v_hbm, pace_ref, surplus_ref,
    acc, scale_ref, final_ref,
    qs, ks, vs, crow, erow, krow, dblock, first, local, theirs, prior, before, after, give,
    dec, dec_theirs, fsend, frecv, squares,
    load_sem, dec_sem, l_send, l_recv, p_send, p_recv, x_send, x_recv,
    f_send, f_recv, s_send, s_recv,
):
    tokens = q_hbm.shape[0]
    blocks = tokens // BLOCK
    chunks = heads // group
    wide = group * HEAD_DIM
    groups = n // 2
    rows = HEAD_DIM // n
    piece = max(rows, 8)
    me = lax.axis_index("seq")
    place = lax.axis_index("tp")
    g, r = me // 2, me % 2
    other = 1 - r
    partner = 2 * g + other

    def owner(s):
        top = s * rows
        return ((top // piece) * 2 * piece + r * piece + top % piece) // rows

    def halves(x):
        return [
            jnp.concatenate(
                [x[at : at + piece] for at in range(p * piece, HEAD_DIM, 2 * piece)], axis=0
            )
            for p in range(2)
        ]

    def joined(a, b):
        return jnp.concatenate(
            [x[at : at + piece] for at in range(0, HALF, piece) for x in (a, b)], axis=0
        )

    is_first, is_last = g == 0, g == groups - 1

    barrier = pltpu.get_barrier_semaphore()
    for step in range(1, n):
        pl.semaphore_signal(
            barrier, inc=1, device_id={"seq": lax.rem(me + step, n)}, device_id_type=MESH
        )
    for step in range(1, peers):
        pl.semaphore_signal(
            barrier, inc=1, device_id={"tp": lax.rem(place + step, peers)}, device_id_type=MESH
        )

    def lanes(i):
        return pl.ds(pl.multiple_of(i * wide, wide), wide)

    def load(which, i):
        source = (k_hbm, v_hbm, q_hbm)[which]
        target = (ks, vs, qs)[which]
        return pltpu.make_async_copy(
            source.at[:, lanes(i)], target.at[i], load_sem.at[which, i]
        )

    def span(i):
        return pl.ds(i * group, group)

    many = heads // 2

    def batch(i):
        return pl.ds(i * many, many)

    def send_dec():
        return pltpu.make_async_remote_copy(
            src_ref=dec, dst_ref=dec_theirs, send_sem=dec_sem.at[0], recv_sem=dec_sem.at[1],
            device_id={"seq": partner}, device_id_type=MESH,
        )

    def send_local(i):
        return pltpu.make_async_remote_copy(
            src_ref=local.at[other, span(i)], dst_ref=theirs.at[span(i)],
            send_sem=l_send.at[i], recv_sem=l_recv.at[i],
            device_id={"seq": partner}, device_id_type=MESH,
        )

    def send_after(i):
        return pltpu.make_async_remote_copy(
            src_ref=after.at[span(i)], dst_ref=before.at[span(i)],
            send_sem=p_send.at[i], recv_sem=p_recv.at[i],
            device_id={"seq": lax.rem(me + 2, n)}, device_id_type=MESH,
        )

    def send_prior(i):
        return pltpu.make_async_remote_copy(
            src_ref=give.at[span(i)], dst_ref=prior.at[r, span(i)],
            send_sem=x_send.at[i], recv_sem=x_recv.at[i],
            device_id={"seq": partner}, device_id_type=MESH,
        )

    def send_final(i, s):
        return pltpu.make_async_remote_copy(
            src_ref=fsend.at[s, batch(i)], dst_ref=frecv.at[batch(i)],
            send_sem=f_send.at[i, s], recv_sem=f_recv.at[i],
            device_id={"seq": owner(s)}, device_id_type=MESH,
        )

    def send_squares(step):
        return pltpu.make_async_remote_copy(
            src_ref=squares.at[0], dst_ref=squares.at[step],
            send_sem=s_send.at[step], recv_sem=s_recv.at[step],
            device_id={"tp": lax.rem(place + step, peers)}, device_id_type=MESH,
        )

    for i in range(chunks):
        load(0, i).start()
        load(1, i).start()

    square = (heads, heads)
    diagonal = lax.broadcasted_iota(jnp.int32, square, 0) == lax.broadcasted_iota(
        jnp.int32, square, 1
    )
    pace = jnp.sum(
        jnp.where(diagonal, jnp.broadcast_to(pace_ref[...], square), 0.0), axis=1, keepdims=True
    )
    logrows = surplus_ref[...] - pace
    upper = (
        lax.broadcasted_iota(jnp.int32, (BLOCK, BLOCK), 0)
        <= lax.broadcasted_iota(jnp.int32, (BLOCK, BLOCK), 1)
    ).astype(F32)
    total = jnp.zeros((heads, 1), F32)
    for b in range(blocks):
        at = slice(b * BLOCK, (b + 1) * BLOCK)
        c = lax.dot_general(
            logrows[:, at], upper, (((1,), (0,)), ((), ())),
            precision=lax.Precision.HIGHEST, preferred_element_type=F32,
        )
        last = c[:, BLOCK - 1 :]
        crow[:, at] = c * LOG2E
        erow[:, at] = jnp.exp(c)
        krow[:, at] = jnp.exp(last - c)
        total = total + last
        dblock[b] = jnp.exp(jnp.broadcast_to(last, (heads, HEAD_DIM)))
    decay = jnp.exp(jnp.broadcast_to(total, (heads, HEAD_DIM)))
    for h in range(heads):
        dec[h] = decay[h : h + 1, :]

    @pl.when(is_first)
    def _():
        before[...] = jnp.zeros_like(before)

        @pl.when(r == 0)
        def _():
            prior[1] = jnp.zeros(prior.shape[1:], F32)

    def make_local(lump):
        for e in range(4):
            h = lump * 4 + e
            load(0, h).wait()
            load(1, h).wait()
            load(2, h).start()
        for e in range(4):
            h = lump * 4 + e
            row = krow[pl.ds(h, 1), :]
            state = None
            for b in range(blocks):
                at = slice(b * BLOCK, (b + 1) * BLOCK)
                kt = ks[h, at, :].astype(F32).T
                both = jnp.dot(
                    split(kt * row[:, at], 0), vs[h, at, :], preferred_element_type=F32
                )
                fresh = both[:HEAD_DIM] + both[HEAD_DIM:]
                state = fresh if b == 0 else dblock[b, pl.ds(h, 1), :] * state + fresh
                if b < blocks - 1:
                    first[b, h] = state
            local[0, h], local[1, h] = halves(state)

    def give_local(lump, carry):
        make_local(lump)
        for e in range(4):
            send_local(lump * 4 + e).start()
        return carry

    make_local(0)
    pl.semaphore_wait(barrier, n + peers - 2)
    for e in range(4):
        send_local(e).start()
    send_dec().start()
    lax.fori_loop(1, heads // 4, give_local, 0)
    send_dec().wait_recv()

    hold = jnp.maximum(chunks // 2 - 3 * g, 0)

    def chain(i):
        send_local(i).wait_recv()

        @pl.when(jnp.logical_not(is_first))
        def _():
            send_after(i).wait_recv()

        at = span(i)
        mine, their = local[r, at], theirs[at]
        d_mine, d_their = dec[at], dec_theirs[at]
        came = before[at]
        even = r == 0
        grown = d_mine * d_their * came + jnp.where(
            even, d_their * mine + their, d_mine * their + mine
        )
        after[at] = grown

        @pl.when(jnp.logical_not(is_last))
        def _():
            send_after(i).start()

        prior[r, at] = jnp.where(even, came, d_their * came + their)

        give[at] = jnp.where(even, d_mine * came + mine, came)

        @pl.when(jnp.logical_not(is_first & (r == 1)))
        def _():
            @pl.when(i >= hold)
            def _():
                send_prior(i - hold).start()

            @pl.when(i == chunks - 1)
            def _():
                def rest(t, carry):
                    @pl.when(t >= chunks - hold)
                    def _():
                        send_prior(t).start()

                    return carry

                lax.fori_loop(0, chunks, rest, 0)

        @pl.when(is_last)
        def _():
            for s in range(groups):
                fsend[s, at] = grown[:, s * rows : (s + 1) * rows, :]

            @pl.when(i % many == many - 1)
            def _():
                part = i // many

                def give_final(s, carry):
                    @pl.when(owner(s) != me)
                    def _():
                        send_final(part, s).start()

                    @pl.when(owner(s) == me)
                    def _():
                        frecv[batch(part)] = fsend[s, batch(part)]

                    return carry

                lax.fori_loop(0, groups, give_final, 0)

    side = BLOCK // 2
    lower = lax.broadcasted_iota(jnp.int32, (side, side), 0) >= lax.broadcasted_iota(
        jnp.int32, (side, side), 1
    )

    def intra(i):
        for e in range(2):
            load(2, i * 2 + e).wait()
        for e in range(2):
            h = i * 2 + e
            row = crow[pl.ds(h, 1), :]
            column = jnp.broadcast_to(row, (side, tokens)).T
            for b in range(blocks):
                at = slice(b * BLOCK, (b + 1) * BLOCK)
                scores = lax.dot_general(
                    qs[h, at, :], ks[h, at, :], (((1,), (1,)), ((), ())),
                    preferred_element_type=F32,
                )

                def weights(t, s):
                    rise = column[b * BLOCK + t : b * BLOCK + t + side, :] - (
                        row[:, b * BLOCK + s : b * BLOCK + s + side]
                    )
                    factor = jnp.exp2(rise)
                    if t == s:
                        factor = jnp.where(lower, factor, 0.0)
                    return (scores[t : t + side, s : s + side] * factor).astype(BF16)

                acc[h, b * BLOCK : b * BLOCK + side, :] = jnp.dot(
                    weights(0, 0), vs[h, b * BLOCK : b * BLOCK + side, :],
                    preferred_element_type=F32,
                )
                acc[h, b * BLOCK + side : (b + 1) * BLOCK, :] = jnp.dot(
                    jnp.concatenate([weights(side, 0), weights(side, side)], axis=1),
                    vs[h, at, :], preferred_element_type=F32,
                )

    lumps = heads // 4
    lag = jnp.minimum(g, lumps)

    def middle(j, carry):
        @pl.when((j >= lag) & (j - lag < lumps))
        def _():
            def step(e, carry):
                chain((j - lag) * 4 + e)
                return carry

            lax.fori_loop(0, 4, step, 0)

        @pl.when(j < heads // 2)
        def _():
            intra(j)

        return carry

    lax.fori_loop(0, max(heads // 2, lumps + min(groups - 1, lumps)), middle, 0)

    def carried(i, sums):
        @pl.when(jnp.logical_not(is_first & (r == 0)))
        def _():
            for e in range(2):
                send_prior(i * 2 + e).wait_recv()

        for e in range(2):
            h = i * 2 + e
            start = joined(prior[0, h], prior[1, h])
            grows = jnp.broadcast_to(erow[pl.ds(h, 1), :], (HEAD_DIM, tokens)).T
            decayed = None
            parts = []
            for b in range(blocks):
                at = slice(b * BLOCK, (b + 1) * BLOCK)
                if b == 0:
                    state = start
                else:
                    state = decayed * start + first[b - 1, h]
                grow = grows[at]
                last = dblock[b, pl.ds(h, 1), :]
                decayed = last if b == 0 else decayed * last
                qb = qs[h, at, :]
                inter = jnp.dot(
                    jnp.concatenate([qb, qb], axis=1), split(state, 0),
                    preferred_element_type=F32,
                )
                out = acc[h, at, :] + grow * inter
                acc[h, at, :] = out
                parts.append(out * out)
            sums = sums + jnp.concatenate(parts, axis=0)
        return sums

    sums = lax.fori_loop(0, heads // 2, carried, jnp.zeros((tokens, HEAD_DIM), F32))
    squares[0] = jnp.sum(sums.T, axis=0, keepdims=True)
    for step in range(1, peers):
        send_squares(step).start()
    for step in range(1, peers):
        send_squares(step).wait_recv()
    whole = squares[0]
    for step in range(1, peers):
        whole = whole + squares[step]
    scale = lax.rsqrt(whole / D + EPS)
    scale_ref[...] = scale

    def drain(i, carry):
        send_local(i).wait_send()

        @pl.when(jnp.logical_not(is_last))
        def _():
            send_after(i).wait_send()

        @pl.when(jnp.logical_not(is_first & (r == 1)))
        def _():
            send_prior(i).wait_send()

        return carry

    lax.fori_loop(0, chunks, drain, 0)

    def drain_final(part, carry):
        @pl.when(is_last)
        def _():
            def sent(s, carry):
                @pl.when(owner(s) != me)
                def _():
                    send_final(part, s).wait_send()

                return carry

            lax.fori_loop(0, groups, sent, 0)

        @pl.when(jnp.logical_not(is_last & ((me * rows // piece) % 2 == r)))
        def _():
            send_final(part, 0).wait_recv()

        return carry

    lax.fori_loop(0, 2, drain_final, 0)
    send_dec().wait_send()
    for step in range(1, peers):
        send_squares(step).wait_send()
    final_ref[...] = frecv[...]


def norm_kernel(acc, scale_ref, gain_ref, final_in, out_hbm, final_ref, outs, store_sem):
    heads, tokens = acc.shape[:2]
    rows = final_in.shape[1]
    wide = outs.shape[2]
    group = wide // HEAD_DIM
    scale = jnp.broadcast_to(scale_ref[...], (HEAD_DIM, tokens)).T

    def store(i):
        return pltpu.make_async_copy(
            outs.at[i], out_hbm.at[:, pl.ds(pl.multiple_of(i * wide, wide), wide)], store_sem.at[i]
        )

    def finish(i, carry):
        for e in range(group):
            h = i * group + e
            gain = gain_ref[:, pl.ds(pl.multiple_of(h * HEAD_DIM, HEAD_DIM), HEAD_DIM)]
            outs[i, :, e * HEAD_DIM : (e + 1) * HEAD_DIM] = (acc[h] * scale * gain).astype(BF16)
        store(i).start()
        return carry

    lax.fori_loop(0, heads // group, finish, 0)
    for at in range(rows):
        final_ref[:, at * HEAD_DIM : (at + 1) * HEAD_DIM] = final_in[:, at, :]

    def drain(i, carry):
        store(i).wait()
        return carry

    lax.fori_loop(0, heads // group, drain, 0)


def on_device(n, peers, q, k, v, pace, surplus, gain):
    tokens, width = q.shape
    heads = pace.shape[0]
    group = 1
    chunks = heads // group
    blocks = tokens // BLOCK
    groups = n // 2
    rows = HEAD_DIM // n
    vmem = pltpu.VMEM
    dma = pltpu.SemaphoreType.DMA
    half = (heads, HALF, HEAD_DIM)
    flops = 2 * heads * tokens * HEAD_DIM * (2 * BLOCK + 4 * HEAD_DIM)
    acc, scale, final = pl.pallas_call(
        functools.partial(kernel, n, peers, heads, group),
        out_shape=(
            vmem((heads, tokens, HEAD_DIM), F32),
            vmem((1, tokens), F32),
            vmem((heads, rows, HEAD_DIM), F32),
        ),
        in_specs=[pl.BlockSpec(memory_space=pl.ANY)] * 3
        + [pl.BlockSpec(memory_space=pltpu.VMEM)] * 2,
        out_specs=[pl.BlockSpec(memory_space=pltpu.VMEM)] * 3,
        scratch_shapes=[
            vmem((chunks, tokens, group * HEAD_DIM), BF16),
            vmem((chunks, tokens, group * HEAD_DIM), BF16),
            vmem((chunks, tokens, group * HEAD_DIM), BF16),
            vmem((heads, tokens), F32),
            vmem((heads, tokens), F32),
            vmem((heads, tokens), F32),
            vmem((blocks, heads, HEAD_DIM), F32),
            vmem((max(blocks - 1, 1), heads, HEAD_DIM, HEAD_DIM), F32),
            vmem((2,) + half, F32),
            vmem(half, F32),
            vmem((2,) + half, F32),
            vmem(half, F32),
            vmem(half, F32),
            vmem(half, F32),
            vmem((heads, 1, HEAD_DIM), F32),
            vmem((heads, 1, HEAD_DIM), F32),
            vmem((groups, heads, rows, HEAD_DIM), F32),
            vmem((heads, rows, HEAD_DIM), F32),
            vmem((peers, 1, tokens), F32),
            dma((3, chunks)),
            dma((2,)),
            dma((chunks,)),
            dma((chunks,)),
            dma((chunks,)),
            dma((chunks,)),
            dma((chunks,)),
            dma((chunks,)),
            dma((2, groups)),
            dma((2,)),
            dma((peers,)),
            dma((peers,)),
        ],
        compiler_params=pltpu.CompilerParams(
            collective_id=0, has_side_effects=True, vmem_limit_bytes=58 * 1024 * 1024
        ),
        cost_estimate=pl.CostEstimate(
            flops=flops, bytes_accessed=8 * tokens * width, transcendentals=heads * tokens * BLOCK
        ),
        name="chained_attention",
    )(q, k, v, pace.reshape(1, heads), surplus.T)
    return pl.pallas_call(
        norm_kernel,
        out_shape=(
            jax.ShapeDtypeStruct((tokens, width), BF16),
            jax.ShapeDtypeStruct((heads, rows * HEAD_DIM), F32),
        ),
        in_specs=[pl.BlockSpec(memory_space=pltpu.VMEM)] * 4,
        out_specs=(
            pl.BlockSpec(memory_space=pl.ANY),
            pl.BlockSpec(memory_space=pltpu.VMEM),
        ),
        scratch_shapes=[vmem((heads // 2, tokens, 2 * HEAD_DIM), BF16), dma((heads // 2,))],
        compiler_params=pltpu.CompilerParams(vmem_limit_bytes=16 * 1024 * 1024),
        cost_estimate=pl.CostEstimate(
            flops=3 * tokens * width, bytes_accessed=6 * tokens * width, transcendentals=0
        ),
        name="norm",
    )(acc, scale, gain.reshape(1, width), final)


def solution(mesh):
    in_specs = (P("seq", "tp"), P("seq", "tp"), P("seq", "tp"), P("tp"), P("seq", "tp"), P("tp"))
    out_specs = (P("seq", "tp"), P("tp", "seq"))
    return jax.shard_map(
        functools.partial(on_device, mesh.shape["seq"], mesh.shape["tp"]),
        mesh=mesh, in_specs=in_specs, out_specs=out_specs, check_vma=False,
    )
```

```python
import functools

import jax
import jax.numpy as jnp
from jax import lax
from jax.experimental import pallas as pl
from jax.experimental.pallas import tpu as pltpu
from jax.sharding import PartitionSpec as P

HEAD_DIM = 128
HALF = HEAD_DIM // 2
BLOCK = 256
D = 8192
EPS = 1e-06
LOG2E = 1.4426950408889634
F32 = jnp.float32
BF16 = jnp.bfloat16
MESH = pl.DeviceIdType.MESH


def split(x, axis):
    high = x.astype(BF16)
    low = (x - high.astype(F32)).astype(BF16)
    return jnp.concatenate([high, low], axis=axis)


def kernel(
    n, peers, heads, group,
    q_hbm, k_hbm, v_hbm, pace_ref, surplus_ref,
    acc, scale_ref, final_ref,
    qs, ks, vs, crow, erow, krow, dblock, first, local, theirs, prior, before, after, give,
    dec, dec_theirs, fsend, frecv, squares,
    load_sem, dec_sem, l_send, l_recv, p_send, p_recv, x_send, x_recv,
    f_send, f_recv, s_send, s_recv,
):
    tokens = q_hbm.shape[0]
    blocks = tokens // BLOCK
    chunks = heads // group
    wide = group * HEAD_DIM
    groups = n // 2
    rows = HEAD_DIM // n
    piece = max(rows, 8)
    me = lax.axis_index("seq")
    place = lax.axis_index("tp")
    g, r = me // 2, me % 2
    other = 1 - r
    partner = 2 * g + other

    def owner(s):
        top = s * rows
        return ((top // piece) * 2 * piece + r * piece + top % piece) // rows

    def halves(x):
        return [
            jnp.concatenate(
                [x[at : at + piece] for at in range(p * piece, HEAD_DIM, 2 * piece)], axis=0
            )
            for p in range(2)
        ]

    def joined(a, b):
        return jnp.concatenate(
            [x[at : at + piece] for at in range(0, HALF, piece) for x in (a, b)], axis=0
        )

    is_first, is_last = g == 0, g == groups - 1

    barrier = pltpu.get_barrier_semaphore()
    for step in range(1, n):
        pl.semaphore_signal(
            barrier, inc=1, device_id={"seq": lax.rem(me + step, n)}, device_id_type=MESH
        )
    for step in range(1, peers):
        pl.semaphore_signal(
            barrier, inc=1, device_id={"tp": lax.rem(place + step, peers)}, device_id_type=MESH
        )

    def lanes(i):
        return pl.ds(pl.multiple_of(i * wide, wide), wide)

    def load(which, i):
        source = (k_hbm, v_hbm, q_hbm)[which]
        target = (ks, vs, qs)[which]
        return pltpu.make_async_copy(
            source.at[:, lanes(i)], target.at[i], load_sem.at[which, i]
        )

    def span(i):
        return pl.ds(i * group, group)

    many = heads // 2

    def batch(i):
        return pl.ds(i * many, many)

    def send_dec():
        return pltpu.make_async_remote_copy(
            src_ref=dec, dst_ref=dec_theirs, send_sem=dec_sem.at[0], recv_sem=dec_sem.at[1],
            device_id={"seq": partner}, device_id_type=MESH,
        )

    def send_local(i):
        return pltpu.make_async_remote_copy(
            src_ref=local.at[other, span(i)], dst_ref=theirs.at[span(i)],
            send_sem=l_send.at[i], recv_sem=l_recv.at[i],
            device_id={"seq": partner}, device_id_type=MESH,
        )

    def send_after(i):
        return pltpu.make_async_remote_copy(
            src_ref=after.at[span(i)], dst_ref=before.at[span(i)],
            send_sem=p_send.at[i], recv_sem=p_recv.at[i],
            device_id={"seq": lax.rem(me + 2, n)}, device_id_type=MESH,
        )

    def send_prior(i):
        return pltpu.make_async_remote_copy(
            src_ref=give.at[span(i)], dst_ref=prior.at[r, span(i)],
            send_sem=x_send.at[i], recv_sem=x_recv.at[i],
            device_id={"seq": partner}, device_id_type=MESH,
        )

    def send_final(i, s):
        return pltpu.make_async_remote_copy(
            src_ref=fsend.at[s, batch(i)], dst_ref=frecv.at[batch(i)],
            send_sem=f_send.at[i, s], recv_sem=f_recv.at[i],
            device_id={"seq": owner(s)}, device_id_type=MESH,
        )

    def send_squares(step):
        return pltpu.make_async_remote_copy(
            src_ref=squares.at[0], dst_ref=squares.at[step],
            send_sem=s_send.at[step], recv_sem=s_recv.at[step],
            device_id={"tp": lax.rem(place + step, peers)}, device_id_type=MESH,
        )

    for i in range(chunks):
        load(0, i).start()
        load(1, i).start()

    square = (heads, heads)
    diagonal = lax.broadcasted_iota(jnp.int32, square, 0) == lax.broadcasted_iota(
        jnp.int32, square, 1
    )
    pace = jnp.sum(
        jnp.where(diagonal, jnp.broadcast_to(pace_ref[...], square), 0.0), axis=1, keepdims=True
    )
    logrows = surplus_ref[...] - pace
    upper = (
        lax.broadcasted_iota(jnp.int32, (BLOCK, BLOCK), 0)
        <= lax.broadcasted_iota(jnp.int32, (BLOCK, BLOCK), 1)
    ).astype(F32)
    total = jnp.zeros((heads, 1), F32)
    for b in range(blocks):
        at = slice(b * BLOCK, (b + 1) * BLOCK)
        c = lax.dot_general(
            logrows[:, at], upper, (((1,), (0,)), ((), ())),
            precision=lax.Precision.HIGHEST, preferred_element_type=F32,
        )
        last = c[:, BLOCK - 1 :]
        crow[:, at] = c * LOG2E
        erow[:, at] = jnp.exp(c)
        krow[:, at] = jnp.exp(last - c)
        total = total + last
        dblock[b] = jnp.exp(jnp.broadcast_to(last, (heads, HEAD_DIM)))
    decay = jnp.exp(jnp.broadcast_to(total, (heads, HEAD_DIM)))
    for h in range(heads):
        dec[h] = decay[h : h + 1, :]

    @pl.when(is_first)
    def _():
        before[...] = jnp.zeros_like(before)

        @pl.when(r == 0)
        def _():
            prior[1] = jnp.zeros(prior.shape[1:], F32)

    def make_local(lump):
        for e in range(4):
            h = lump * 4 + e
            load(0, h).wait()
            load(1, h).wait()
            load(2, h).start()
        for e in range(4):
            h = lump * 4 + e
            row = krow[pl.ds(h, 1), :]
            state = None
            for b in range(blocks):
                at = slice(b * BLOCK, (b + 1) * BLOCK)
                kt = ks[h, at, :].astype(F32).T
                both = jnp.dot(
                    split(kt * row[:, at], 0), vs[h, at, :], preferred_element_type=F32
                )
                fresh = both[:HEAD_DIM] + both[HEAD_DIM:]
                state = fresh if b == 0 else dblock[b, pl.ds(h, 1), :] * state + fresh
                if b < blocks - 1:
                    first[b, h] = state
            local[0, h], local[1, h] = halves(state)

    def give_local(lump, carry):
        make_local(lump)
        for e in range(4):
            send_local(lump * 4 + e).start()
        return carry

    make_local(0)
    pl.semaphore_wait(barrier, n + peers - 2)
    for e in range(4):
        send_local(e).start()
    send_dec().start()
    lax.fori_loop(1, heads // 4, give_local, 0)
    send_dec().wait_recv()

    hold = jnp.maximum(3 * chunks // 4 - 3 * g, 0)

    def chain(i):
        send_local(i).wait_recv()

        @pl.when(jnp.logical_not(is_first))
        def _():
            send_after(i).wait_recv()

        at = span(i)
        mine, their = local[r, at], theirs[at]
        d_mine, d_their = dec[at], dec_theirs[at]
        came = before[at]
        even = r == 0
        grown = d_mine * d_their * came + jnp.where(
            even, d_their * mine + their, d_mine * their + mine
        )
        after[at] = grown

        @pl.when(jnp.logical_not(is_last))
        def _():
            send_after(i).start()

        prior[r, at] = jnp.where(even, came, d_their * came + their)

        give[at] = jnp.where(even, d_mine * came + mine, came)

        @pl.when(jnp.logical_not(is_first & (r == 1)))
        def _():
            @pl.when(i >= hold)
            def _():
                send_prior(i - hold).start()

            @pl.when(i == chunks - 1)
            def _():
                def rest(t, carry):
                    @pl.when(t >= chunks - hold)
                    def _():
                        send_prior(t).start()

                    return carry

                lax.fori_loop(0, chunks, rest, 0)

        @pl.when(is_last)
        def _():
            for s in range(groups):
                fsend[s, at] = grown[:, s * rows : (s + 1) * rows, :]

            @pl.when(i % many == many - 1)
            def _():
                part = i // many

                def give_final(s, carry):
                    @pl.when(owner(s) != me)
                    def _():
                        send_final(part, s).start()

                    @pl.when(owner(s) == me)
                    def _():
                        frecv[batch(part)] = fsend[s, batch(part)]

                    return carry

                lax.fori_loop(0, groups, give_final, 0)

    side = BLOCK // 2
    lower = lax.broadcasted_iota(jnp.int32, (side, side), 0) >= lax.broadcasted_iota(
        jnp.int32, (side, side), 1
    )

    def intra(i):
        for e in range(2):
            load(2, i * 2 + e).wait()
        for e in range(2):
            h = i * 2 + e
            row = crow[pl.ds(h, 1), :]
            column = jnp.broadcast_to(row, (side, tokens)).T
            for b in range(blocks):
                at = slice(b * BLOCK, (b + 1) * BLOCK)
                scores = lax.dot_general(
                    qs[h, at, :], ks[h, at, :], (((1,), (1,)), ((), ())),
                    preferred_element_type=F32,
                )

                def weights(t, s):
                    rise = column[b * BLOCK + t : b * BLOCK + t + side, :] - (
                        row[:, b * BLOCK + s : b * BLOCK + s + side]
                    )
                    factor = jnp.exp2(rise)
                    if t == s:
                        factor = jnp.where(lower, factor, 0.0)
                    return (scores[t : t + side, s : s + side] * factor).astype(BF16)

                acc[h, b * BLOCK : b * BLOCK + side, :] = jnp.dot(
                    weights(0, 0), vs[h, b * BLOCK : b * BLOCK + side, :],
                    preferred_element_type=F32,
                )
                acc[h, b * BLOCK + side : (b + 1) * BLOCK, :] = jnp.dot(
                    jnp.concatenate([weights(side, 0), weights(side, side)], axis=1),
                    vs[h, at, :], preferred_element_type=F32,
                )

    lumps = heads // 4
    lag = jnp.minimum(2 * g, 2 * lumps)

    def middle(j, carry):
        @pl.when((j >= lag) & (j - lag < lumps))
        def _():
            def step(e, carry):
                chain((j - lag) * 4 + e)
                return carry

            lax.fori_loop(0, 4, step, 0)

        @pl.when(j < heads // 2)
        def _():
            intra(j)

        return carry

    lax.fori_loop(0, max(heads // 2, lumps + min(2 * (groups - 1), 2 * lumps)), middle, 0)

    def carried(i, sums):
        @pl.when(jnp.logical_not(is_first & (r == 0)))
        def _():
            for e in range(2):
                send_prior(i * 2 + e).wait_recv()

        for e in range(2):
            h = i * 2 + e
            start = joined(prior[0, h], prior[1, h])
            grows = jnp.broadcast_to(erow[pl.ds(h, 1), :], (HEAD_DIM, tokens)).T
            decayed = None
            parts = []
            for b in range(blocks):
                at = slice(b * BLOCK, (b + 1) * BLOCK)
                if b == 0:
                    state = start
                else:
                    state = decayed * start + first[b - 1, h]
                grow = grows[at]
                last = dblock[b, pl.ds(h, 1), :]
                decayed = last if b == 0 else decayed * last
                qb = qs[h, at, :]
                inter = jnp.dot(
                    jnp.concatenate([qb, qb], axis=1), split(state, 0),
                    preferred_element_type=F32,
                )
                out = acc[h, at, :] + grow * inter
                acc[h, at, :] = out
                parts.append(out * out)
            sums = sums + jnp.concatenate(parts, axis=0)
        return sums

    sums = lax.fori_loop(0, heads // 2, carried, jnp.zeros((tokens, HEAD_DIM), F32))
    squares[0] = jnp.sum(sums.T, axis=0, keepdims=True)
    for step in range(1, peers):
        send_squares(step).start()
    for step in range(1, peers):
        send_squares(step).wait_recv()
    whole = squares[0]
    for step in range(1, peers):
        whole = whole + squares[step]
    scale = lax.rsqrt(whole / D + EPS)
    scale_ref[...] = scale

    def drain(i, carry):
        send_local(i).wait_send()

        @pl.when(jnp.logical_not(is_last))
        def _():
            send_after(i).wait_send()

        @pl.when(jnp.logical_not(is_first & (r == 1)))
        def _():
            send_prior(i).wait_send()

        return carry

    lax.fori_loop(0, chunks, drain, 0)

    def drain_final(part, carry):
        @pl.when(is_last)
        def _():
            def sent(s, carry):
                @pl.when(owner(s) != me)
                def _():
                    send_final(part, s).wait_send()

                return carry

            lax.fori_loop(0, groups, sent, 0)

        @pl.when(jnp.logical_not(is_last & ((me * rows // piece) % 2 == r)))
        def _():
            send_final(part, 0).wait_recv()

        return carry

    lax.fori_loop(0, 2, drain_final, 0)
    send_dec().wait_send()
    for step in range(1, peers):
        send_squares(step).wait_send()
    final_ref[...] = frecv[...]


def norm_kernel(acc, scale_ref, gain_ref, final_in, out_hbm, final_ref, outs, store_sem):
    heads, tokens = acc.shape[:2]
    rows = final_in.shape[1]
    wide = outs.shape[2]
    group = wide // HEAD_DIM
    scale = jnp.broadcast_to(scale_ref[...], (HEAD_DIM, tokens)).T

    def store(i):
        return pltpu.make_async_copy(
            outs.at[i], out_hbm.at[:, pl.ds(pl.multiple_of(i * wide, wide), wide)], store_sem.at[i]
        )

    def finish(i, carry):
        for e in range(group):
            h = i * group + e
            gain = gain_ref[:, pl.ds(pl.multiple_of(h * HEAD_DIM, HEAD_DIM), HEAD_DIM)]
            outs[i, :, e * HEAD_DIM : (e + 1) * HEAD_DIM] = (acc[h] * scale * gain).astype(BF16)
        store(i).start()
        return carry

    lax.fori_loop(0, heads // group, finish, 0)
    for at in range(rows):
        final_ref[:, at * HEAD_DIM : (at + 1) * HEAD_DIM] = final_in[:, at, :]

    def drain(i, carry):
        store(i).wait()
        return carry

    lax.fori_loop(0, heads // group, drain, 0)


def on_device(n, peers, q, k, v, pace, surplus, gain):
    tokens, width = q.shape
    heads = pace.shape[0]
    group = 1
    chunks = heads // group
    blocks = tokens // BLOCK
    groups = n // 2
    rows = HEAD_DIM // n
    vmem = pltpu.VMEM
    dma = pltpu.SemaphoreType.DMA
    half = (heads, HALF, HEAD_DIM)
    flops = 2 * heads * tokens * HEAD_DIM * (2 * BLOCK + 4 * HEAD_DIM)
    acc, scale, final = pl.pallas_call(
        functools.partial(kernel, n, peers, heads, group),
        out_shape=(
            vmem((heads, tokens, HEAD_DIM), F32),
            vmem((1, tokens), F32),
            vmem((heads, rows, HEAD_DIM), F32),
        ),
        in_specs=[pl.BlockSpec(memory_space=pl.ANY)] * 3
        + [pl.BlockSpec(memory_space=pltpu.VMEM)] * 2,
        out_specs=[pl.BlockSpec(memory_space=pltpu.VMEM)] * 3,
        scratch_shapes=[
            vmem((chunks, tokens, group * HEAD_DIM), BF16),
            vmem((chunks, tokens, group * HEAD_DIM), BF16),
            vmem((chunks, tokens, group * HEAD_DIM), BF16),
            vmem((heads, tokens), F32),
            vmem((heads, tokens), F32),
            vmem((heads, tokens), F32),
            vmem((blocks, heads, HEAD_DIM), F32),
            vmem((max(blocks - 1, 1), heads, HEAD_DIM, HEAD_DIM), F32),
            vmem((2,) + half, F32),
            vmem(half, F32),
            vmem((2,) + half, F32),
            vmem(half, F32),
            vmem(half, F32),
            vmem(half, F32),
            vmem((heads, 1, HEAD_DIM), F32),
            vmem((heads, 1, HEAD_DIM), F32),
            vmem((groups, heads, rows, HEAD_DIM), F32),
            vmem((heads, rows, HEAD_DIM), F32),
            vmem((peers, 1, tokens), F32),
            dma((3, chunks)),
            dma((2,)),
            dma((chunks,)),
            dma((chunks,)),
            dma((chunks,)),
            dma((chunks,)),
            dma((chunks,)),
            dma((chunks,)),
            dma((2, groups)),
            dma((2,)),
            dma((peers,)),
            dma((peers,)),
        ],
        compiler_params=pltpu.CompilerParams(
            collective_id=0, has_side_effects=True, vmem_limit_bytes=58 * 1024 * 1024
        ),
        cost_estimate=pl.CostEstimate(
            flops=flops, bytes_accessed=8 * tokens * width, transcendentals=heads * tokens * BLOCK
        ),
        name="chained_attention",
    )(q, k, v, pace.reshape(1, heads), surplus.T)
    return pl.pallas_call(
        norm_kernel,
        out_shape=(
            jax.ShapeDtypeStruct((tokens, width), BF16),
            jax.ShapeDtypeStruct((heads, rows * HEAD_DIM), F32),
        ),
        in_specs=[pl.BlockSpec(memory_space=pltpu.VMEM)] * 4,
        out_specs=(
            pl.BlockSpec(memory_space=pl.ANY),
            pl.BlockSpec(memory_space=pltpu.VMEM),
        ),
        scratch_shapes=[vmem((heads // 2, tokens, 2 * HEAD_DIM), BF16), dma((heads // 2,))],
        compiler_params=pltpu.CompilerParams(vmem_limit_bytes=16 * 1024 * 1024),
        cost_estimate=pl.CostEstimate(
            flops=3 * tokens * width, bytes_accessed=6 * tokens * width, transcendentals=0
        ),
        name="norm",
    )(acc, scale, gain.reshape(1, width), final)


def solution(mesh):
    in_specs = (P("seq", "tp"), P("seq", "tp"), P("seq", "tp"), P("tp"), P("seq", "tp"), P("tp"))
    out_specs = (P("seq", "tp"), P("tp", "seq"))
    return jax.shard_map(
        functools.partial(on_device, mesh.shape["seq"], mesh.shape["tp"]),
        mesh=mesh, in_specs=in_specs, out_specs=out_specs, check_vma=False,
    )
```

```python
import functools

import jax
import jax.numpy as jnp
from jax import lax
from jax.experimental import pallas as pl
from jax.experimental.pallas import tpu as pltpu
from jax.sharding import PartitionSpec as P

HEAD_DIM = 128
HALF = HEAD_DIM // 2
BLOCK = 256
D = 8192
EPS = 1e-06
LOG2E = 1.4426950408889634
F32 = jnp.float32
BF16 = jnp.bfloat16
MESH = pl.DeviceIdType.MESH


def split(x, axis):
    high = x.astype(BF16)
    low = (x - high.astype(F32)).astype(BF16)
    return jnp.concatenate([high, low], axis=axis)


def kernel(
    n, peers, heads, group,
    q_hbm, k_hbm, v_hbm, pace_ref, surplus_ref,
    acc, scale_ref, final_ref,
    qs, ks, vs, crow, erow, krow, dblock, first, local, theirs, prior, before, after, give,
    dec, dec_theirs, fsend, frecv, squares,
    load_sem, dec_sem, l_send, l_recv, p_send, p_recv, x_send, x_recv,
    f_send, f_recv, s_send, s_recv,
):
    tokens = q_hbm.shape[0]
    blocks = tokens // BLOCK
    chunks = heads // group
    wide = group * HEAD_DIM
    groups = n // 2
    rows = HEAD_DIM // n
    piece = max(rows, 8)
    me = lax.axis_index("seq")
    place = lax.axis_index("tp")
    g, r = me // 2, me % 2
    other = 1 - r
    partner = 2 * g + other

    def owner(s):
        top = s * rows
        return ((top // piece) * 2 * piece + r * piece + top % piece) // rows

    def halves(x):
        return [
            jnp.concatenate(
                [x[at : at + piece] for at in range(p * piece, HEAD_DIM, 2 * piece)], axis=0
            )
            for p in range(2)
        ]

    def joined(a, b):
        return jnp.concatenate(
            [x[at : at + piece] for at in range(0, HALF, piece) for x in (a, b)], axis=0
        )

    is_first, is_last = g == 0, g == groups - 1

    barrier = pltpu.get_barrier_semaphore()
    for step in range(1, n):
        pl.semaphore_signal(
            barrier, inc=1, device_id={"seq": lax.rem(me + step, n)}, device_id_type=MESH
        )
    for step in range(1, peers):
        pl.semaphore_signal(
            barrier, inc=1, device_id={"tp": lax.rem(place + step, peers)}, device_id_type=MESH
        )

    def lanes(i):
        return pl.ds(pl.multiple_of(i * wide, wide), wide)

    def load(which, i):
        source = (k_hbm, v_hbm, q_hbm)[which]
        target = (ks, vs, qs)[which]
        return pltpu.make_async_copy(
            source.at[:, lanes(i)], target.at[i], load_sem.at[which, i]
        )

    def span(i):
        return pl.ds(i * group, group)

    many = heads // 2

    def batch(i):
        return pl.ds(i * many, many)

    def send_dec():
        return pltpu.make_async_remote_copy(
            src_ref=dec, dst_ref=dec_theirs, send_sem=dec_sem.at[0], recv_sem=dec_sem.at[1],
            device_id={"seq": partner}, device_id_type=MESH,
        )

    def send_local(i):
        return pltpu.make_async_remote_copy(
            src_ref=local.at[other, span(i)], dst_ref=theirs.at[span(i)],
            send_sem=l_send.at[i], recv_sem=l_recv.at[i],
            device_id={"seq": partner}, device_id_type=MESH,
        )

    def send_after(i):
        return pltpu.make_async_remote_copy(
            src_ref=after.at[span(i)], dst_ref=before.at[span(i)],
            send_sem=p_send.at[i], recv_sem=p_recv.at[i],
            device_id={"seq": lax.rem(me + 2, n)}, device_id_type=MESH,
        )

    def send_prior(i):
        return pltpu.make_async_remote_copy(
            src_ref=give.at[span(i)], dst_ref=prior.at[r, span(i)],
            send_sem=x_send.at[i], recv_sem=x_recv.at[i],
            device_id={"seq": partner}, device_id_type=MESH,
        )

    def send_final(i, s):
        return pltpu.make_async_remote_copy(
            src_ref=fsend.at[s, batch(i)], dst_ref=frecv.at[batch(i)],
            send_sem=f_send.at[i, s], recv_sem=f_recv.at[i],
            device_id={"seq": owner(s)}, device_id_type=MESH,
        )

    def send_squares(step):
        return pltpu.make_async_remote_copy(
            src_ref=squares.at[0], dst_ref=squares.at[step],
            send_sem=s_send.at[step], recv_sem=s_recv.at[step],
            device_id={"tp": lax.rem(place + step, peers)}, device_id_type=MESH,
        )

    for i in range(chunks):
        load(0, i).start()
        load(1, i).start()

    square = (heads, heads)
    diagonal = lax.broadcasted_iota(jnp.int32, square, 0) == lax.broadcasted_iota(
        jnp.int32, square, 1
    )
    pace = jnp.sum(
        jnp.where(diagonal, jnp.broadcast_to(pace_ref[...], square), 0.0), axis=1, keepdims=True
    )
    logrows = surplus_ref[...] - pace
    upper = (
        lax.broadcasted_iota(jnp.int32, (BLOCK, BLOCK), 0)
        <= lax.broadcasted_iota(jnp.int32, (BLOCK, BLOCK), 1)
    ).astype(F32)
    total = jnp.zeros((heads, 1), F32)
    for b in range(blocks):
        at = slice(b * BLOCK, (b + 1) * BLOCK)
        c = lax.dot_general(
            logrows[:, at], upper, (((1,), (0,)), ((), ())),
            precision=lax.Precision.HIGHEST, preferred_element_type=F32,
        )
        last = c[:, BLOCK - 1 :]
        crow[:, at] = c * LOG2E
        erow[:, at] = jnp.exp(c)
        krow[:, at] = jnp.exp(last - c)
        total = total + last
        dblock[b] = jnp.exp(jnp.broadcast_to(last, (heads, HEAD_DIM)))
    decay = jnp.exp(jnp.broadcast_to(total, (heads, HEAD_DIM)))
    for h in range(heads):
        dec[h] = decay[h : h + 1, :]

    @pl.when(is_first)
    def _():
        before[...] = jnp.zeros_like(before)

        @pl.when(r == 0)
        def _():
            prior[1] = jnp.zeros(prior.shape[1:], F32)

    def make_local(lump):
        for e in range(4):
            h = lump * 4 + e
            load(0, h).wait()
            load(1, h).wait()
            load(2, h).start()
        for e in range(4):
            h = lump * 4 + e
            row = krow[pl.ds(h, 1), :]
            state = None
            for b in range(blocks):
                at = slice(b * BLOCK, (b + 1) * BLOCK)
                kt = ks[h, at, :].astype(F32).T
                both = jnp.dot(
                    split(kt * row[:, at], 0), vs[h, at, :], preferred_element_type=F32
                )
                fresh = both[:HEAD_DIM] + both[HEAD_DIM:]
                state = fresh if b == 0 else dblock[b, pl.ds(h, 1), :] * state + fresh
                if b < blocks - 1:
                    first[b, h] = state
            local[0, h], local[1, h] = halves(state)

    def give_local(lump, carry):
        make_local(lump)
        for e in range(4):
            send_local(lump * 4 + e).start()
        return carry

    make_local(0)
    pl.semaphore_wait(barrier, n + peers - 2)
    for e in range(4):
        send_local(e).start()
    send_dec().start()
    lax.fori_loop(1, heads // 4, give_local, 0)
    send_dec().wait_recv()

    hold = jnp.maximum(chunks // 2 - 3 * g, 0)

    def chain(i):
        send_local(i).wait_recv()

        @pl.when(jnp.logical_not(is_first))
        def _():
            send_after(i).wait_recv()

        at = span(i)
        mine, their = local[r, at], theirs[at]
        d_mine, d_their = dec[at], dec_theirs[at]
        came = before[at]
        even = r == 0
        grown = d_mine * d_their * came + jnp.where(
            even, d_their * mine + their, d_mine * their + mine
        )
        after[at] = grown

        @pl.when(jnp.logical_not(is_last))
        def _():
            send_after(i).start()

        prior[r, at] = jnp.where(even, came, d_their * came + their)

        give[at] = jnp.where(even, d_mine * came + mine, came)

        @pl.when(jnp.logical_not(is_first & (r == 1)))
        def _():
            @pl.when(i >= hold)
            def _():
                send_prior(i - hold).start()

            @pl.when(i == chunks - 1)
            def _():
                def rest(t, carry):
                    @pl.when(t >= chunks - hold)
                    def _():
                        send_prior(t).start()

                    return carry

                lax.fori_loop(0, chunks, rest, 0)

        @pl.when(is_last)
        def _():
            for s in range(groups):
                fsend[s, at] = grown[:, s * rows : (s + 1) * rows, :]

            @pl.when(i % many == many - 1)
            def _():
                part = i // many

                def give_final(s, carry):
                    @pl.when(owner(s) != me)
                    def _():
                        send_final(part, s).start()

                    @pl.when(owner(s) == me)
                    def _():
                        frecv[batch(part)] = fsend[s, batch(part)]

                    return carry

                lax.fori_loop(0, groups, give_final, 0)

    side = BLOCK // 2
    lower = lax.broadcasted_iota(jnp.int32, (side, side), 0) >= lax.broadcasted_iota(
        jnp.int32, (side, side), 1
    )

    def intra(i):
        for e in range(2):
            load(2, i * 2 + e).wait()
        for e in range(2):
            h = i * 2 + e
            row = crow[pl.ds(h, 1), :]
            column = jnp.broadcast_to(row, (side, tokens)).T
            for b in range(blocks):
                at = slice(b * BLOCK, (b + 1) * BLOCK)
                scores = lax.dot_general(
                    qs[h, at, :], ks[h, at, :], (((1,), (1,)), ((), ())),
                    preferred_element_type=F32,
                )

                def weights(t, s):
                    rise = column[b * BLOCK + t : b * BLOCK + t + side, :] - (
                        row[:, b * BLOCK + s : b * BLOCK + s + side]
                    )
                    factor = jnp.exp2(rise)
                    if t == s:
                        factor = jnp.where(lower, factor, 0.0)
                    return (scores[t : t + side, s : s + side] * factor).astype(BF16)

                acc[h, b * BLOCK : b * BLOCK + side, :] = jnp.dot(
                    weights(0, 0), vs[h, b * BLOCK : b * BLOCK + side, :],
                    preferred_element_type=F32,
                )
                acc[h, b * BLOCK + side : (b + 1) * BLOCK, :] = jnp.dot(
                    jnp.concatenate([weights(side, 0), weights(side, side)], axis=1),
                    vs[h, at, :], preferred_element_type=F32,
                )

    lumps = heads // 4
    lag = jnp.minimum(g, lumps) + jnp.where(is_last, 2, 0)

    def middle(j, carry):
        @pl.when((j >= lag) & (j - lag < lumps))
        def _():
            def step(e, carry):
                chain((j - lag) * 4 + e)
                return carry

            lax.fori_loop(0, 4, step, 0)

        @pl.when(j < heads // 2)
        def _():
            intra(j)

        return carry

    lax.fori_loop(0, max(heads // 2, lumps + 2 + min(groups - 1, lumps)), middle, 0)

    def carried(i, sums):
        @pl.when(jnp.logical_not(is_first & (r == 0)))
        def _():
            for e in range(2):
                send_prior(i * 2 + e).wait_recv()

        for e in range(2):
            h = i * 2 + e
            start = joined(prior[0, h], prior[1, h])
            grows = jnp.broadcast_to(erow[pl.ds(h, 1), :], (HEAD_DIM, tokens)).T
            decayed = None
            parts = []
            for b in range(blocks):
                at = slice(b * BLOCK, (b + 1) * BLOCK)
                if b == 0:
                    state = start
                else:
                    state = decayed * start + first[b - 1, h]
                grow = grows[at]
                last = dblock[b, pl.ds(h, 1), :]
                decayed = last if b == 0 else decayed * last
                qb = qs[h, at, :]
                inter = jnp.dot(
                    jnp.concatenate([qb, qb], axis=1), split(state, 0),
                    preferred_element_type=F32,
                )
                out = acc[h, at, :] + grow * inter
                acc[h, at, :] = out
                parts.append(out * out)
            sums = sums + jnp.concatenate(parts, axis=0)
        return sums

    sums = lax.fori_loop(0, heads // 2, carried, jnp.zeros((tokens, HEAD_DIM), F32))
    squares[0] = jnp.sum(sums.T, axis=0, keepdims=True)
    for step in range(1, peers):
        send_squares(step).start()
    for step in range(1, peers):
        send_squares(step).wait_recv()
    whole = squares[0]
    for step in range(1, peers):
        whole = whole + squares[step]
    scale = lax.rsqrt(whole / D + EPS)
    scale_ref[...] = scale

    def drain(i, carry):
        send_local(i).wait_send()

        @pl.when(jnp.logical_not(is_last))
        def _():
            send_after(i).wait_send()

        @pl.when(jnp.logical_not(is_first & (r == 1)))
        def _():
            send_prior(i).wait_send()

        return carry

    lax.fori_loop(0, chunks, drain, 0)

    def drain_final(part, carry):
        @pl.when(is_last)
        def _():
            def sent(s, carry):
                @pl.when(owner(s) != me)
                def _():
                    send_final(part, s).wait_send()

                return carry

            lax.fori_loop(0, groups, sent, 0)

        @pl.when(jnp.logical_not(is_last & ((me * rows // piece) % 2 == r)))
        def _():
            send_final(part, 0).wait_recv()

        return carry

    lax.fori_loop(0, 2, drain_final, 0)
    send_dec().wait_send()
    for step in range(1, peers):
        send_squares(step).wait_send()
    final_ref[...] = frecv[...]


def norm_kernel(acc, scale_ref, gain_ref, final_in, out_hbm, final_ref, outs, store_sem):
    heads, tokens = acc.shape[:2]
    rows = final_in.shape[1]
    wide = outs.shape[2]
    group = wide // HEAD_DIM
    scale = jnp.broadcast_to(scale_ref[...], (HEAD_DIM, tokens)).T

    def store(i):
        return pltpu.make_async_copy(
            outs.at[i], out_hbm.at[:, pl.ds(pl.multiple_of(i * wide, wide), wide)], store_sem.at[i]
        )

    def finish(i, carry):
        for e in range(group):
            h = i * group + e
            gain = gain_ref[:, pl.ds(pl.multiple_of(h * HEAD_DIM, HEAD_DIM), HEAD_DIM)]
            outs[i, :, e * HEAD_DIM : (e + 1) * HEAD_DIM] = (acc[h] * scale * gain).astype(BF16)
        store(i).start()
        return carry

    lax.fori_loop(0, heads // group, finish, 0)
    for at in range(rows):
        final_ref[:, at * HEAD_DIM : (at + 1) * HEAD_DIM] = final_in[:, at, :]

    def drain(i, carry):
        store(i).wait()
        return carry

    lax.fori_loop(0, heads // group, drain, 0)


def on_device(n, peers, q, k, v, pace, surplus, gain):
    tokens, width = q.shape
    heads = pace.shape[0]
    group = 1
    chunks = heads // group
    blocks = tokens // BLOCK
    groups = n // 2
    rows = HEAD_DIM // n
    vmem = pltpu.VMEM
    dma = pltpu.SemaphoreType.DMA
    half = (heads, HALF, HEAD_DIM)
    flops = 2 * heads * tokens * HEAD_DIM * (2 * BLOCK + 4 * HEAD_DIM)
    acc, scale, final = pl.pallas_call(
        functools.partial(kernel, n, peers, heads, group),
        out_shape=(
            vmem((heads, tokens, HEAD_DIM), F32),
            vmem((1, tokens), F32),
            vmem((heads, rows, HEAD_DIM), F32),
        ),
        in_specs=[pl.BlockSpec(memory_space=pl.ANY)] * 3
        + [pl.BlockSpec(memory_space=pltpu.VMEM)] * 2,
        out_specs=[pl.BlockSpec(memory_space=pltpu.VMEM)] * 3,
        scratch_shapes=[
            vmem((chunks, tokens, group * HEAD_DIM), BF16),
            vmem((chunks, tokens, group * HEAD_DIM), BF16),
            vmem((chunks, tokens, group * HEAD_DIM), BF16),
            vmem((heads, tokens), F32),
            vmem((heads, tokens), F32),
            vmem((heads, tokens), F32),
            vmem((blocks, heads, HEAD_DIM), F32),
            vmem((max(blocks - 1, 1), heads, HEAD_DIM, HEAD_DIM), F32),
            vmem((2,) + half, F32),
            vmem(half, F32),
            vmem((2,) + half, F32),
            vmem(half, F32),
            vmem(half, F32),
            vmem(half, F32),
            vmem((heads, 1, HEAD_DIM), F32),
            vmem((heads, 1, HEAD_DIM), F32),
            vmem((groups, heads, rows, HEAD_DIM), F32),
            vmem((heads, rows, HEAD_DIM), F32),
            vmem((peers, 1, tokens), F32),
            dma((3, chunks)),
            dma((2,)),
            dma((chunks,)),
            dma((chunks,)),
            dma((chunks,)),
            dma((chunks,)),
            dma((chunks,)),
            dma((chunks,)),
            dma((2, groups)),
            dma((2,)),
            dma((peers,)),
            dma((peers,)),
        ],
        compiler_params=pltpu.CompilerParams(
            collective_id=0, has_side_effects=True, vmem_limit_bytes=58 * 1024 * 1024
        ),
        cost_estimate=pl.CostEstimate(
            flops=flops, bytes_accessed=8 * tokens * width, transcendentals=heads * tokens * BLOCK
        ),
        name="chained_attention",
    )(q, k, v, pace.reshape(1, heads), surplus.T)
    return pl.pallas_call(
        norm_kernel,
        out_shape=(
            jax.ShapeDtypeStruct((tokens, width), BF16),
            jax.ShapeDtypeStruct((heads, rows * HEAD_DIM), F32),
        ),
        in_specs=[pl.BlockSpec(memory_space=pltpu.VMEM)] * 4,
        out_specs=(
            pl.BlockSpec(memory_space=pl.ANY),
            pl.BlockSpec(memory_space=pltpu.VMEM),
        ),
        scratch_shapes=[vmem((heads // 2, tokens, 2 * HEAD_DIM), BF16), dma((heads // 2,))],
        compiler_params=pltpu.CompilerParams(vmem_limit_bytes=16 * 1024 * 1024),
        cost_estimate=pl.CostEstimate(
            flops=3 * tokens * width, bytes_accessed=6 * tokens * width, transcendentals=0
        ),
        name="norm",
    )(acc, scale, gain.reshape(1, width), final)


def solution(mesh):
    in_specs = (P("seq", "tp"), P("seq", "tp"), P("seq", "tp"), P("tp"), P("seq", "tp"), P("tp"))
    out_specs = (P("seq", "tp"), P("tp", "seq"))
    return jax.shard_map(
        functools.partial(on_device, mesh.shape["seq"], mesh.shape["tp"]),
        mesh=mesh, in_specs=in_specs, out_specs=out_specs, check_vma=False,
    )
```
